32 devices in a mesh: groups: 2 (over x), gx: 16 (over z, y, core).
Axes of the slice: x: 2, y: 2, z: 4, core: 2. Of those that a mesh axis runs over, the one named last changes fastest.
Arguments:
- hidden_in: bfloat16 [704, 8192], P('groups', 'gx'), parts along dimension 0, may hold values from -22 to 22
- norm_gain: float32 [8192], P('gx'), may hold values from 0.4 to 1.6
- w_qkv: bfloat16 [8192, 10240], P('gx'), may hold values from -0.0625 to 0.0625
- w_out: bfloat16 [8192, 8192], P(None, 'gx'), may hold values from -0.0625 to 0.0625
- cache_keys: bfloat16 [704, 128, 1024], P(('groups', 'gx')), parts along dimension 0, may hold values from -34 to 34
- cache_values: bfloat16 [704, 128, 1024], P(('groups', 'gx')), parts along dimension 0, may hold values from -6 to 6
- lengths: int32 [704], P(('groups', 'gx')), parts along dimension 0, may hold values from 1 to 128, as said below
Outputs:
- hidden_out: bfloat16 [704, 8192], P('groups', 'gx'), parts along dimension 0
The draws below stay inside these ranges and needn't reach their ends.
There are 2 independent parts, one for each index of `groups`. The reference program is written for one: setup_inputs(seed, part) draws one part's arguments, and reference() takes and returns one part's arrays. A program takes and returns all parts, laid end to end along the dimension named above; an argument that names none is the same for every part. Nothing has to cross between parts.
Inputs may be any that keep to these rules, and one draw needn't show every extreme that they name: `lengths`: each sequence's length lies between 1 and 128; the first sequence of each replica has 128.
All inputs are finite; a program needn't handle non-finite values.
Results may differ from the reference program's by a relative error of at most 0.014.
Values may be sent and summed in bfloat16 or wider, within the bound.
No kernel may reach another device: no remote copies, remote signals or barrier semaphores. Data moves between devices by JAX's collectives and lax.ppermute only.
A program may use at most 128 MiB of HBM per device.

```python
import jax
import jax.numpy as jnp
from jax import lax

D = 8192
HEADS = 64
KVH = 8
HD = 128
SEQ_DEV = 22
CACHE = 128
SEQS = 352
QKV = 10240
N_GX = 16


def draw_hidden_in(key, part):
    key = jax.random.fold_in(key, 31)
    base_key = jax.random.fold_in(key, 0)
    shape = (SEQS, D)
    place = jnp.arange(D, dtype=jnp.float32) / max(D - 1, 1)
    base = jnp.clip(jax.random.normal(base_key, shape, jnp.float32), -4.0, 4.0)
    rising = 0.5 * jnp.exp(place * jnp.log(5.0))
    return (base * rising[None, :]).astype(jnp.bfloat16)


def draw_cache_keys(key, part):
    key = jax.random.fold_in(key, 11)
    law_key = jax.random.fold_in(key, 2)
    shape = (SEQS, CACHE, KVH * HD)
    base = jax.random.normal(law_key, shape, jnp.float32)
    return jnp.clip(base, -6.0, 6.0).astype(jnp.bfloat16)


def draw_lengths(key, part):
    key = jax.random.fold_in(key, 23)
    cap_key, len_key = jax.random.split(key)
    blocks = SEQS // SEQ_DEV
    caps = jax.random.randint(cap_key, (blocks, 1), max(CACHE // 4, 1), CACHE + 1)
    drawn = jax.random.randint(len_key, (blocks, SEQ_DEV), 1, CACHE + 1)
    drawn = jnp.minimum(drawn, caps)
    flat = drawn.reshape(SEQS).astype(jnp.int32)
    return flat.at[0].set(CACHE)


def levels(key, extent, pieces, low, largest):
    def one(axis_at, shards_of):
        heights = jax.random.uniform(jax.random.fold_in(jax.random.fold_in(key, 6), axis_at), (shards_of,), jnp.float32, low / len(pieces), largest / len(pieces))
        return jnp.repeat(jnp.exp(heights), extent[axis_at] // shards_of).reshape((-1,) + (1,) * (len(extent) - axis_at - 1))

    level = one(*pieces[0])
    for cut in pieces[1:]:
        level = level * one(*cut)
    return level


def scatter_about(stream_key, shape, deviation, most, cuts=(), held_as=jnp.bfloat16):
    values = deviation * jax.random.normal(stream_key, shape, jnp.float32)
    if cuts:
        values = values * levels(stream_key, shape, cuts, -0.22, 0.18)
    return jnp.clip(values, -most, most).astype(held_as)


def setup_inputs(seed: int = 0, part: int = 0) -> dict:
    key_list = jax.random.split(jax.random.key(seed), 8)
    part_keys = jax.random.split(jax.random.fold_in(key_list[7], part), 8)
    hidden_in = draw_hidden_in(jax.random.fold_in(jax.random.fold_in(key_list[7], part), 71), part)
    norm_gain = jnp.clip(1.0 + 0.12 * jax.random.normal(key_list[1], (D,), jnp.float32), 0.4, 1.6)
    w_qkv = scatter_about(key_list[2], (D, QKV), D ** -0.5, 0.0625, ((0, 16),))
    w_out = scatter_about(key_list[3], (HEADS * HD, D), (HEADS * HD) ** -0.5, 0.0625, ((1, 16),))
    cache_keys = draw_cache_keys(jax.random.fold_in(jax.random.fold_in(key_list[7], part), 71), part)
    cache_values = scatter_about(part_keys[5], (SEQS, CACHE, KVH * HD), 1.0, 6.0, ((0, 16),))
    lengths = draw_lengths(jax.random.fold_in(jax.random.fold_in(key_list[7], part), 71), part)
    return {"hidden_in": hidden_in, "norm_gain": norm_gain, "w_qkv": w_qkv, "w_out": w_out, "cache_keys": cache_keys, "cache_values": cache_values, "lengths": lengths}


def rotate(heads, positions):
    half = heads.shape[-1] // 2
    inverse = 500000.0 ** (-(jnp.arange(half, dtype=jnp.float32) * 2.0 / heads.shape[-1]))
    angle = positions.astype(jnp.float32)[:, None] * inverse[None, :]
    cosine = jnp.cos(angle)[:, None, :]
    sine = jnp.sin(angle)[:, None, :]
    first = heads[..., :half]
    second = heads[..., half:]
    return jnp.concatenate([first * cosine - second * sine, second * cosine + first * sine], axis=-1)

def attend(query, key_new, value_new, cache_keys, cache_values, lengths):
    count = query.shape[0]
    slots = cache_keys.shape[1]
    kv_heads = key_new.shape[1]
    size = key_new.shape[2]
    group = query.shape[1] // kv_heads
    scale = 1.0 / size ** 0.5
    grouped = query.reshape(count, kv_heads, group, size).astype(jnp.float32)
    keys = cache_keys.reshape(count, slots, kv_heads, size).astype(jnp.float32)
    values = cache_values.reshape(count, slots, kv_heads, size).astype(jnp.float32)
    scores = jnp.einsum('skgd,slkd->skgl', grouped, keys) * scale
    valid = (jnp.arange(slots, dtype=jnp.int32)[None, :] < lengths[:, None])[:, None, None, :]
    scores = jnp.where(valid, scores, -1e+30)
    own = jnp.einsum('skgd,skd->skg', grouped, key_new.astype(jnp.float32)) * scale
    top = jnp.maximum(lax.optimization_barrier(jnp.max(scores, axis=-1)), own)
    expo = jnp.where(valid, jnp.exp(scores - top[..., None]), 0.0)
    own_expo = jnp.exp(own - top)
    total = lax.optimization_barrier(jnp.sum(expo, axis=-1)) + own_expo
    weights = (expo / total[..., None]).astype(jnp.bfloat16)
    own_weight = (own_expo / total).astype(jnp.bfloat16)
    mixed = jnp.einsum('skgl,slkd->skgd', weights.astype(jnp.float32), values)
    mixed = mixed + own_weight.astype(jnp.float32)[..., None] * value_new.astype(jnp.float32)[:, :, None, :]
    return mixed.astype(jnp.bfloat16).reshape(count, kv_heads * group * size)

def reference(hidden_in, norm_gain, w_qkv, w_out, cache_keys, cache_values, lengths):
    count = hidden_in.shape[0]
    features = hidden_in.astype(jnp.float32)
    mean_square = lax.optimization_barrier(jnp.mean(features * features, axis=1))
    scaled = (features * norm_gain[None, :]).astype(jnp.bfloat16)
    block = D // N_GX
    scaled_blocks = jnp.transpose(scaled.reshape(count, N_GX, block), (1, 0, 2))
    weight_blocks = w_qkv.reshape(N_GX, block, w_qkv.shape[1])

    def add_block(carry, pair):
        rows, weights = pair
        partial_sum = jnp.dot(rows, weights, preferred_element_type=jnp.float32).astype(jnp.bfloat16)
        return (carry + partial_sum.astype(jnp.float32), None)
    start = jnp.zeros((count, w_qkv.shape[1]), jnp.float32)
    projected, unused = lax.scan(add_block, start, (scaled_blocks, weight_blocks))
    projected = projected * lax.rsqrt(mean_square + 1e-05)[:, None]
    width_q = HEADS * HD
    width_k = KVH * HD
    query = projected[:, :width_q].reshape(count, HEADS, HD)
    key_new = projected[:, width_q:width_q + width_k].reshape(count, KVH, HD)
    value_new = projected[:, width_q + width_k:].reshape(count, KVH, HD)
    query = rotate(query, lengths).astype(jnp.bfloat16)
    key_new = rotate(key_new, lengths).astype(jnp.bfloat16)
    value_new = value_new.astype(jnp.bfloat16)
    attended = attend(query, key_new, value_new, cache_keys, cache_values, lengths)
    result = features + jnp.dot(attended, w_out, preferred_element_type=jnp.float32)
    return result.astype(jnp.bfloat16)
```

```python
import functools

import jax
import jax.numpy as jnp
import numpy as np
from jax import lax
from jax.experimental import pallas as pl
from jax.experimental.pallas import tpu as pltpu
from jax.sharding import PartitionSpec as P

D = 8192
HEADS = 64
KVH = 8
HD = 128
GROUP = HEADS // KVH
PARTS = 2
KV_PART = KVH // PARTS
Q_PART = HEADS * HD // PARTS
K_PART = KVH * HD // PARTS
N_PART = Q_PART + 2 * K_PART
MIB = 1 << 20
BF = jnp.bfloat16
F32 = jnp.float32


def chip_cycle(mesh):
    devices = np.moveaxis(mesh.devices, mesh.axis_names.index("gx"), -1)
    devices = devices.reshape(-1, devices.shape[-1])[0][::2]
    count = len(devices)
    places = [getattr(d, "coords", None) for d in devices]
    if any(p is None for p in places):
        return list(range(count))

    def linked(a, b):
        return sum(abs(int(u) - int(v)) for u, v in zip(places[a], places[b])) == 1

    def extend(path):
        if len(path) == count:
            return path if linked(path[-1], path[0]) else None
        for nxt in range(count):
            if nxt not in path and linked(path[-1], nxt):
                found = extend(path + [nxt])
                if found:
                    return found
        return None

    return extend([0]) or list(range(count))


def hops(part, chips):
    far = chips // 2
    near = chips - 1 - far
    return (far, near) if part % 2 == 0 else (near, far)


def offsets(part, chips):
    right, left = hops(part, chips)
    first = [right % chips, -left % chips]
    return first + [k for k in range(chips) if k not in first]


def qkv_kernel(rows, pad, chips, slots_ref, x_ref, gain_ref, w_ref, mine_ref, sib_a_ref, sib_b_ref, xs_ref):
    total = x_ref.shape[0]

    @pl.when(pl.program_id(0) == 0)
    def _():
        scaled = (x_ref[...].astype(F32) * gain_ref[...]).astype(BF)
        me = lax.axis_index("gx")
        row = lax.broadcasted_iota(jnp.int32, (pad, total), 0)
        col = lax.broadcasted_iota(jnp.int32, (pad, total), 1)
        picks = []
        for slot in range(2 * chips):
            start = slots_ref[me, slot] * rows
            picks.append(jnp.where((col == row + start) & (row < rows), 1.0, 0.0))
        pick = jnp.concatenate(picks, axis=0).astype(BF)
        xs_ref[...] = jnp.dot(pick, scaled, preferred_element_type=F32).astype(BF)

    out = jnp.dot(xs_ref[...], w_ref[...], preferred_element_type=F32)
    for slot in range(chips):
        mine_ref[slot] = out[slot * pad : (slot + 1) * pad].astype(BF)
        other = out[(chips + slot) * pad : (chips + slot + 1) * pad].astype(BF)
        if slot < 2:
            sib_a_ref[slot] = other
        else:
            sib_b_ref[slot - 2] = other


def project(part, rows, pad, chips, slots, x, gain, w):
    block = K_PART
    q_blocks = Q_PART // block
    k_first = HEADS * HD // block
    v_first = k_first + KVH * HD // block
    total, depth = x.shape

    def w_index(j, slots_ref):
        q = part * q_blocks + j
        return 0, jnp.where(j < q_blocks, q, jnp.where(j == q_blocks, k_first + part, v_first + part))

    return pl.pallas_call(
        functools.partial(qkv_kernel, rows, pad, chips),
        grid_spec=pltpu.PrefetchScalarGridSpec(
            num_scalar_prefetch=1,
            grid=(N_PART // block,),
            in_specs=[
                pl.BlockSpec((total, depth), lambda j, s: (0, 0)),
                pl.BlockSpec((1, depth), lambda j, s: (0, 0)),
                pl.BlockSpec((depth, block), w_index),
            ],
            out_specs=[
                pl.BlockSpec((chips, pad, block), lambda j, s: (0, 0, j)),
                pl.BlockSpec((2, pad, block), lambda j, s: (0, 0, j)),
                pl.BlockSpec((chips - 2, pad, block), lambda j, s: (0, 0, j)),
            ],
            scratch_shapes=[pltpu.VMEM((2 * chips * pad, depth), BF)],
        ),
        out_shape=[
            jax.ShapeDtypeStruct((chips, pad, N_PART), BF),
            jax.ShapeDtypeStruct((2, pad, N_PART), BF),
            jax.ShapeDtypeStruct((chips - 2, pad, N_PART), BF),
        ],
        compiler_params=pltpu.CompilerParams(vmem_limit_bytes=24 * MIB),
        cost_estimate=pl.CostEstimate(
            flops=2 * 2 * chips * pad * depth * N_PART, bytes_accessed=depth * N_PART * 2 + 2 * chips * pad * N_PART * 2, transcendentals=0
        ),
        name="qkv_part",
    )(slots, x, gain, w)


def attend_kernel(rows, pad, own_ref, sib_ref, left_ref, right_ref, inv_ref, cos_ref, sin_ref, len_ref, k_ref, v_ref, out_ref, s_ref, m_ref):
    live = rows * GROUP
    full = pad * GROUP
    slots = k_ref.shape[1]
    scale = 1.0 / HD**0.5
    inv = inv_ref[...]
    cos = cos_ref[...]
    sin = sin_ref[...]

    def tile(t):
        lanes = slice(t * HD, (t + 1) * HD)
        got = own_ref[0, :, lanes].astype(F32) + sib_ref[0, :, lanes].astype(F32)
        got = got + (left_ref[0, :, lanes].astype(F32) + right_ref[0, :, lanes].astype(F32))
        return got * inv

    def turned(t):
        a = tile(t)
        return (a * cos + pltpu.roll(a, HD // 2, 1) * sin).astype(BF)

    r = lax.broadcasted_iota(jnp.int32, (full, full), 0)
    c = lax.broadcasted_iota(jnp.int32, (full, full), 1)
    by_seq = jnp.where(c == (r % GROUP) * pad + r // GROUP, 1.0, 0.0).astype(BF)
    by_head = jnp.where(r == (c % GROUP) * pad + c // GROUP, 1.0, 0.0).astype(BF)
    r2 = lax.broadcasted_iota(jnp.int32, (full, pad), 0)
    c2 = lax.broadcasted_iota(jnp.int32, (full, pad), 1)
    spread = jnp.where(c2 == r2 // GROUP, 1.0, 0.0).astype(BF)
    valid = lax.broadcasted_iota(jnp.int32, (live, slots), 1) < len_ref[...]

    for kk in range(KV_PART):
        q = jnp.concatenate([turned(kk * GROUP + g).astype(F32) for g in range(GROUP)], axis=0).astype(BF)
        q = jnp.dot(by_seq, q, preferred_element_type=F32)
        k_new = jnp.dot(spread, turned(KV_PART * GROUP + kk), preferred_element_type=F32)
        v_new = jnp.dot(spread, tile(KV_PART * GROUP + KV_PART + kk).astype(BF), preferred_element_type=F32)
        own = (jnp.sum(q * k_new, axis=1, keepdims=True) * scale)[:live]
        lanes = slice(kk * HD, (kk + 1) * HD)
        for s in range(rows):
            s_ref[s * GROUP : (s + 1) * GROUP] = lax.dot_general(
                q[s * GROUP : (s + 1) * GROUP].astype(BF),
                k_ref[s, :, lanes],
                (((1,), (1,)), ((), ())),
                preferred_element_type=F32,
            )
        scores = jnp.where(valid, s_ref[...] * scale, -1e30)
        top = jnp.maximum(jnp.max(scores, axis=1, keepdims=True), own)
        expo = jnp.where(valid, jnp.exp(scores - top), 0.0)
        own_expo = jnp.exp(own - top)
        total = jnp.sum(expo, axis=1, keepdims=True) + own_expo
        s_ref[...] = expo / total
        own_weight = (own_expo / total).astype(BF).astype(F32)
        for s in range(rows):
            m_ref[s * GROUP : (s + 1) * GROUP] = jnp.dot(
                s_ref[s * GROUP : (s + 1) * GROUP].astype(BF), v_ref[s, :, lanes], preferred_element_type=F32
            )
        mixed = m_ref[...] + own_weight * v_new[:live]
        mixed = jnp.concatenate([mixed, jnp.zeros((full - live, HD), F32)], axis=0).astype(BF)
        mixed = jnp.dot(by_head, mixed, preferred_element_type=F32)
        for g in range(GROUP):
            out_ref[:, (kk * GROUP + g) * HD : (kk * GROUP + g + 1) * HD] = mixed[g * pad : (g + 1) * pad].astype(BF)


def attend(part, rows, pad, mine, sib, at, from_left, from_right, inv, cos, sin, lens, keys, values):
    slots = keys.shape[1]
    at_mine, at_sib = at
    return pl.pallas_call(
        functools.partial(attend_kernel, rows, pad),
        grid=(1,),
        in_specs=[
            pl.BlockSpec((1, pad, N_PART), lambda i: (at_mine, 0, 0)),
            pl.BlockSpec((1, pad, N_PART), lambda i: (at_sib, 0, 0)),
            pl.BlockSpec((1, pad, N_PART), lambda i: (0, 0, 0)),
            pl.BlockSpec((1, pad, N_PART), lambda i: (0, 0, 0)),
            pl.BlockSpec((pad, HD), lambda i: (0, 0)),
            pl.BlockSpec((pad, HD), lambda i: (0, 0)),
            pl.BlockSpec((pad, HD), lambda i: (0, 0)),
            pl.BlockSpec((rows * GROUP, 1), lambda i: (0, 0)),
            pl.BlockSpec((rows, slots, K_PART), lambda i: (0, 0, part)),
            pl.BlockSpec((rows, slots, K_PART), lambda i: (0, 0, part)),
        ],
        out_specs=pl.BlockSpec((pad, Q_PART), lambda i: (0, 0)),
        out_shape=jax.ShapeDtypeStruct((pad, Q_PART), BF),
        scratch_shapes=[pltpu.VMEM((rows * GROUP, slots), F32), pltpu.VMEM((rows * GROUP, HD), F32)],
        compiler_params=pltpu.CompilerParams(vmem_limit_bytes=32 * MIB),
        cost_estimate=pl.CostEstimate(
            flops=4 * rows * KV_PART * GROUP * slots * HD * 16, bytes_accessed=4 * rows * slots * K_PART * 2, transcendentals=rows * 32 * slots
        ),
        name="attend_part",
    )(mine, sib, from_left, from_right, inv, cos, sin, lens, keys, values)


def out_kernel(rows, pad, count, last, slots_ref, *refs):
    blocks = refs[:count]
    w_ref = refs[count]
    rest = refs[count + 1 :]
    if last:
        x_ref, prior_ref, out_ref, acc_ref, a_ref = rest
    else:
        out_ref, acc_ref, a_ref = rest
    step = pl.program_id(0)
    for b in range(count):
        a_ref[b * pad : (b + 1) * pad] = blocks[b][...].astype(F32)
    prod = jnp.dot(a_ref[...].astype(BF), w_ref[...], preferred_element_type=F32)

    @pl.when(step == 0)
    def _():
        acc_ref[...] = prod + prior_ref[...] if last else prod

    @pl.when(step > 0)
    def _():
        acc_ref[...] += prod

    @pl.when(step == pl.num_programs(0) - 1)
    def _():
        if not last:
            out_ref[...] = acc_ref[...]
            return
        total = x_ref.shape[0]
        me = lax.axis_index("gx")
        row = lax.broadcasted_iota(jnp.int32, (pad, total), 0)
        col = lax.broadcasted_iota(jnp.int32, (pad, total), 1)
        picks = []
        for slot in range(count):
            start = slots_ref[me, slot] * rows
            picks.append(jnp.where((col == row + start) & (row < rows), 1.0, 0.0))
        pick = jnp.concatenate(picks, axis=0).astype(BF)
        features = jnp.dot(pick, x_ref[...], preferred_element_type=F32)
        result = (features + acc_ref[...]).astype(BF)
        out_ref[...] = lax.dot_general(pick, result, (((0,), (0,)), ((), ())), preferred_element_type=F32).astype(BF)


def project_out(part, rows, pad, slots, blocks, w, x=None, prior=None):
    count = len(blocks)
    cols = w.shape[1]
    block = 1024
    steps = Q_PART // block
    last = prior is not None
    in_specs = [pl.BlockSpec((pad, block), lambda k, s: (0, k)) for _ in blocks]
    in_specs.append(pl.BlockSpec((block, cols), lambda k, s: (part * steps + k, 0)))
    args = list(blocks) + [w]
    if last:
        in_specs += [pl.BlockSpec(x.shape, lambda k, s: (0, 0)), pl.BlockSpec((count * pad, cols), lambda k, s: (0, 0))]
        args += [x, prior]
        out_shape = jax.ShapeDtypeStruct((x.shape[0], cols), BF)
    else:
        out_shape = jax.ShapeDtypeStruct((count * pad, cols), F32)
    return pl.pallas_call(
        functools.partial(out_kernel, rows, pad, count, last),
        grid_spec=pltpu.PrefetchScalarGridSpec(
            num_scalar_prefetch=1,
            grid=(steps,),
            in_specs=in_specs,
            out_specs=pl.BlockSpec(out_shape.shape, lambda k, s: (0, 0)),
            scratch_shapes=[pltpu.VMEM((count * pad, cols), F32), pltpu.VMEM((count * pad, block), F32)],
        ),
        out_shape=out_shape,
        compiler_params=pltpu.CompilerParams(vmem_limit_bytes=24 * MIB),
        cost_estimate=pl.CostEstimate(
            flops=2 * count * pad * Q_PART * cols, bytes_accessed=Q_PART * cols * 2 + count * pad * Q_PART * 2, transcendentals=0
        ),
        name="out_part",
    )(slots, *args)


def wide(a):
    return a.astype(F32)


def per_device(order, hidden_in, norm_gain, w_qkv, w_out, cache_keys, cache_values, lengths):
    rows = cache_keys.shape[0]
    pad = -(-rows // 8) * 8
    chips = len(order)
    count = 2 * chips
    place = {chip: p for p, chip in enumerate(order)}

    def shift(step):
        return [(order[p] * 2 + c, order[(p + step) % chips] * 2 + c) for p in range(chips) for c in range(2)]

    to_right, to_left, to_core = shift(1), shift(-1), [(i, i ^ 1) for i in range(count)]

    def slot_table(ks):
        table = np.zeros((count, count), np.int32)
        for dev in range(count):
            p, core = place[dev // 2], dev % 2
            for j, k in enumerate(ks):
                target = order[(p + k) % chips] * 2
                table[dev, j] = target + core
                table[dev, chips + j] = target + 1 - core
        return jnp.asarray(table)

    def move(a, pairs):
        return lax.ppermute(a, "gx", pairs)

    features = wide(hidden_in)
    square = jnp.sum(features * features, axis=1)
    bit = 1
    while bit < count:
        square = square + move(square, [(i, i ^ bit) for i in range(count)])
        bit *= 2
    square_own = lax.dynamic_slice_in_dim(square, lax.axis_index("gx") * rows, rows, 0)
    inverse_rms = jnp.pad(lax.rsqrt(square_own / D + 1e-05), (0, pad - rows))
    inv = jnp.broadcast_to(inverse_rms[:, None], (pad, HD))

    half = HD // 2
    inverse = 500000.0 ** (-(jnp.arange(half, dtype=F32) * 2.0 / HD))
    angle = jnp.pad(lengths, (0, pad - rows)).astype(F32)[:, None] * inverse[None, :]
    cos = jnp.cos(angle)
    sin = jnp.sin(angle)
    cos = jnp.concatenate([cos, cos], axis=1)
    sin = jnp.concatenate([-sin, sin], axis=1)
    lens = jnp.repeat(lengths, GROUP)[:, None]

    gain = norm_gain[None, :]
    attended = []
    for part in range(PARTS):
        ks = offsets(part, chips)
        mine, sib_a, sib_b = project(part, rows, pad, chips, slot_table(ks), hidden_in, gain, w_qkv)
        got_a = move(sib_a, to_core)
        got_b = move(sib_b, to_core)

        def terms(k):
            j = ks.index(k % chips)
            return wide(mine[j : j + 1]) + wide(got_a[j : j + 1] if j < 2 else got_b[j - 2 : j - 1])

        right, left = hops(part, chips)
        from_left = move(terms(right).astype(BF), to_right)
        from_right = move(terms(-left).astype(BF), to_left)
        for step in range(1, max(right, left)):
            if step < right:
                from_left = move((terms(right - step) + wide(from_left)).astype(BF), to_right)
            if step < left:
                from_right = move((terms(step - left) + wide(from_right)).astype(BF), to_left)
        at = ks.index(0)
        attended.append(
            attend(part, rows, pad, mine, got_b, (at, at - 2), from_left, from_right, inv, cos, sin, lens, cache_keys, cache_values)
        )

    total = None
    for part in range(PARTS):
        right, left = hops(part, chips)
        blocks = {0: attended[part]}
        for step in range(max(right, left)):
            if step < right:
                blocks[-(step + 1) % chips] = move(blocks[-step % chips], to_right)
            if step < left:
                blocks[step + 1] = move(blocks[step], to_left)
        ks = list(range(chips))
        ordered = [blocks[k] for k in ks] + [move(blocks[k], to_core) for k in ks]
        if part < PARTS - 1:
            total = project_out(part, rows, pad, slot_table(ks), ordered, w_out)
        else:
            total = project_out(part, rows, pad, slot_table(ks), ordered, w_out, hidden_in, total)
    return total


def solution(mesh):
    in_specs = (
        P("groups", "gx"),
        P("gx"),
        P("gx", None),
        P(None, "gx"),
        P(("groups", "gx"), None, None),
        P(("groups", "gx"), None, None),
        P(("groups", "gx")),
    )
    out_specs = P("groups", "gx")
    return jax.shard_map(
        functools.partial(per_device, chip_cycle(mesh)), mesh=mesh, in_specs=in_specs, out_specs=out_specs, check_vma=False
    )
```

```python
import functools

import jax
import jax.numpy as jnp
import numpy as np
from jax import lax
from jax.experimental import pallas as pl
from jax.experimental.pallas import tpu as pltpu
from jax.sharding import PartitionSpec as P

D = 8192
HEADS = 64
KVH = 8
HD = 128
GROUP = HEADS // KVH
PARTS = ((0, 4), (4, 4))
MIB = 1 << 20
BF = jnp.bfloat16
F32 = jnp.float32


def chip_cycle(mesh):
    devices = np.moveaxis(mesh.devices, mesh.axis_names.index("gx"), -1)
    devices = devices.reshape(-1, devices.shape[-1])[0][::2]
    count = len(devices)
    places = [getattr(d, "coords", None) for d in devices]
    if any(p is None for p in places):
        return list(range(count))

    def linked(a, b):
        return sum(abs(int(u) - int(v)) for u, v in zip(places[a], places[b])) == 1

    def extend(path):
        if len(path) == count:
            return path if linked(path[-1], path[0]) else None
        for nxt in range(count):
            if nxt not in path and linked(path[-1], nxt):
                found = extend(path + [nxt])
                if found:
                    return found
        return None

    return extend([0]) or list(range(count))


def hops(index, chips):
    far = chips // 2
    near = chips - 1 - far
    return (far, near) if index % 2 == 0 else (near, far)


def sent_slots(index, chips):
    up, down = hops(index, chips)
    first = [up, chips - down]
    ks = first + [k for k in range(chips) if k not in first]
    return [(k, 0) for k in ks] + [(k, 1) for k in ks]


def gathered_slots(chips):
    return [(k, w) for w in (0, 1) for k in range(chips)]


def slot_devices(order, slots):
    chips = len(order)
    me = lax.axis_index("gx")
    chip, core = me // 2, me % 2
    place = sum(jnp.where(chip == c, p, 0) for p, c in enumerate(order))

    def chip_at(distance):
        at = (place + distance) % chips
        return sum(jnp.where(at == p, c, 0) for p, c in enumerate(order))

    at = {m: chip_at(m) for m in sorted({m for m, _ in slots})}
    return [at[m] * 2 + jnp.where(core == w, 0, 1) for m, w in slots]


def picker(order, slots, rows, pad, total):
    row = lax.broadcasted_iota(jnp.int32, (pad, total), 0)
    col = lax.broadcasted_iota(jnp.int32, (pad, total), 1)
    picks = [jnp.where((col == row + dev * rows) & (row < rows), 1.0, 0.0) for dev in slot_devices(order, slots)]
    return jnp.concatenate(picks, axis=0).astype(BF)


def qkv_kernel(order, index, rows, pad, x_ref, gain_ref, w_ref, keep_ref, first_ref, rest_ref, xs_ref, w_buf, in_sem):
    total, depth = x_ref.shape
    begin, heads = PARTS[index]
    piece = heads * HD
    pieces = GROUP + 2
    firsts = [begin * GROUP * HD + j * piece for j in range(GROUP)]
    firsts += [(HEADS + begin) * HD, (HEADS + KVH + begin) * HD]
    slots = sent_slots(index, len(order))
    kept, first = keep_ref.shape[0], first_ref.shape[0]
    ahead = 4

    def load(j):
        return pltpu.make_async_copy(w_ref.at[:, pl.ds(firsts[j], piece)], w_buf.at[j], in_sem.at[j])

    def write(slot, lanes, value):
        if slot < kept:
            keep_ref[slot, :, lanes] = value
        elif slot < kept + first:
            first_ref[slot - kept, :, lanes] = value
        else:
            rest_ref[slot - kept - first, :, lanes] = value

    for j in range(ahead):
        load(j).start()
    features = jnp.dot(picker(order, slots, rows, pad, total), x_ref[...], preferred_element_type=F32)
    xs_ref[...] = (features * gain_ref[...]).astype(BF)
    width = pieces * piece
    extra = keep_ref.shape[2] - width
    if extra:
        me = lax.axis_index("gx")
        square = jnp.sum(features * features, axis=1, keepdims=True)
        lane = lax.broadcasted_iota(jnp.int32, (len(slots) * pad, extra), 1)
        high = square.astype(BF).astype(F32)
        mid = (square - high).astype(BF).astype(F32)
        low = square - high - mid
        held = jnp.where(lane == 3 * me, high, 0.0) + jnp.where(lane == 3 * me + 1, mid, 0.0) + jnp.where(lane == 3 * me + 2, low, 0.0)
        for slot in range(len(slots)):
            write(slot, slice(width, None), held[slot * pad : (slot + 1) * pad].astype(BF))
    for j in range(pieces):
        if j + ahead < pieces:
            load(j + ahead).start()
        load(j).wait()
        out = jnp.dot(xs_ref[...], w_buf[j], preferred_element_type=F32)
        for slot in range(len(slots)):
            write(slot, slice(j * piece, (j + 1) * piece), out[slot * pad : (slot + 1) * pad].astype(BF))


def project(order, index, rows, pad, x, gain, w):
    piece = PARTS[index][1] * HD
    pieces = GROUP + 2
    depth = x.shape[1]
    chips = len(order)
    extra = -(-6 * chips // 128) * 128 if index == 0 else 0
    width = pieces * piece + extra
    vmem = pl.BlockSpec(memory_space=pltpu.VMEM)
    return pl.pallas_call(
        functools.partial(qkv_kernel, order, index, rows, pad),
        in_specs=[vmem, vmem, pl.BlockSpec(memory_space=pltpu.HBM)],
        out_specs=[vmem] * 3,
        scratch_shapes=[
            pltpu.VMEM((2 * chips * pad, depth), BF),
            pltpu.VMEM((pieces, depth, piece), BF),
            pltpu.SemaphoreType.DMA((pieces,)),
        ],
        out_shape=[jax.ShapeDtypeStruct((n, pad, width), BF) for n in (chips, 2, chips - 2)],
        compiler_params=pltpu.CompilerParams(vmem_limit_bytes=(56 if index == 0 else 46) * MIB),
        cost_estimate=pl.CostEstimate(flops=1, bytes_accessed=1, transcendentals=0),
        name="qkv_part",
    )(x, gain, w)


def attend_kernel(part, rows, pad, own_ref, core_ref, left_ref, right_ref, inv_ref, cos_ref, sin_ref, len_ref, k_ref, v_ref, out_ref, s_ref, m_ref):
    begin, heads = part
    live = rows * GROUP
    full = pad * GROUP
    slots = k_ref.shape[1]
    scale = 1.0 / HD**0.5
    inv = inv_ref[...]
    cos = cos_ref[...]
    sin = sin_ref[...]

    def tile(t):
        lanes = slice(t * HD, (t + 1) * HD)
        got = own_ref[0, :, lanes].astype(F32) + core_ref[0, :, lanes].astype(F32)
        return (got + (left_ref[0, :, lanes].astype(F32) + right_ref[0, :, lanes].astype(F32))) * inv

    def turned(t):
        a = tile(t)
        return (a * cos + pltpu.roll(a, HD // 2, 1) * sin).astype(BF)

    r = lax.broadcasted_iota(jnp.int32, (full, full), 0)
    c = lax.broadcasted_iota(jnp.int32, (full, full), 1)
    by_seq = jnp.where(c == (r % GROUP) * pad + r // GROUP, 1.0, 0.0).astype(BF)
    by_head = jnp.where(r == (c % GROUP) * pad + c // GROUP, 1.0, 0.0).astype(BF)
    r2 = lax.broadcasted_iota(jnp.int32, (full, pad), 0)
    c2 = lax.broadcasted_iota(jnp.int32, (full, pad), 1)
    spread = jnp.where(c2 == r2 // GROUP, 1.0, 0.0).astype(BF)
    valid = lax.broadcasted_iota(jnp.int32, (live, slots), 1) < len_ref[...]

    queries, owns, values_new = [], [], []
    for kk in range(heads):
        q = jnp.concatenate([turned(kk * GROUP + g).astype(F32) for g in range(GROUP)], axis=0).astype(BF)
        q = jnp.dot(by_seq, q, preferred_element_type=F32)
        k_new = jnp.dot(spread, turned(heads * GROUP + kk), preferred_element_type=F32)
        values_new.append(jnp.dot(spread, tile(heads * GROUP + heads + kk).astype(BF), preferred_element_type=F32)[:live])
        owns.append((jnp.sum(q * k_new, axis=1, keepdims=True) * scale)[:live])
        queries.append(q)
    for kk in range(heads):
        lanes = slice((begin + kk) * HD, (begin + kk + 1) * HD)
        for s in range(rows):
            s_ref[kk, s * GROUP : (s + 1) * GROUP] = lax.dot_general(
                queries[kk][s * GROUP : (s + 1) * GROUP].astype(BF),
                k_ref[s, :, lanes],
                (((1,), (1,)), ((), ())),
                preferred_element_type=F32,
            )
    own_weights = []
    for kk in range(heads):
        scores = jnp.where(valid, s_ref[kk] * scale, -1e30)
        top = jnp.maximum(jnp.max(scores, axis=1, keepdims=True), owns[kk])
        expo = jnp.where(valid, jnp.exp(scores - top), 0.0)
        own_expo = jnp.exp(owns[kk] - top)
        total = jnp.sum(expo, axis=1, keepdims=True) + own_expo
        s_ref[kk] = expo / total
        own_weights.append((own_expo / total).astype(BF).astype(F32))
    for kk in range(heads):
        lanes = slice((begin + kk) * HD, (begin + kk + 1) * HD)
        for s in range(rows):
            m_ref[kk, s * GROUP : (s + 1) * GROUP] = jnp.dot(
                s_ref[kk, s * GROUP : (s + 1) * GROUP].astype(BF), v_ref[s, :, lanes], preferred_element_type=F32
            )
    for kk in range(heads):
        mixed = m_ref[kk] + own_weights[kk] * values_new[kk]
        mixed = jnp.concatenate([mixed, jnp.zeros((full - live, HD), F32)], axis=0).astype(BF)
        mixed = jnp.dot(by_head, mixed, preferred_element_type=F32)
        for g in range(GROUP):
            out_ref[0, :, (kk * GROUP + g) * HD : (kk * GROUP + g + 1) * HD] = mixed[g * pad : (g + 1) * pad].astype(BF)


def load(name, limit, arrays, begin=0, count=None):
    count = arrays[0].shape[0] if count is None else count

    def kernel(*refs):
        sems = refs[-1]
        copies = [
            pltpu.make_async_copy(refs[i].at[pl.ds(begin, count)], refs[len(arrays) + i], sems.at[i]) for i in range(len(arrays))
        ]
        for copy in copies:
            copy.start()
        for copy in copies:
            copy.wait()

    return pl.pallas_call(
        kernel,
        in_specs=[pl.BlockSpec(memory_space=pltpu.HBM)] * len(arrays),
        out_specs=[pl.BlockSpec(memory_space=pltpu.VMEM)] * len(arrays),
        out_shape=[jax.ShapeDtypeStruct((count,) + a.shape[1:], BF) for a in arrays],
        scratch_shapes=[pltpu.SemaphoreType.DMA((len(arrays),))],
        compiler_params=pltpu.CompilerParams(vmem_limit_bytes=limit * MIB),
        cost_estimate=pl.CostEstimate(flops=1, bytes_accessed=1, transcendentals=0),
        name=name,
    )(*arrays)


def attend(part, rows, pad, own, from_core, from_left, from_right, inv, cos, sin, lens, keys, values):
    slots = keys.shape[1]
    heads = part[1]
    vmem = pl.BlockSpec(memory_space=pltpu.VMEM)
    return pl.pallas_call(
        functools.partial(attend_kernel, part, rows, pad),
        in_specs=[vmem] * 10,
        out_specs=vmem,
        out_shape=jax.ShapeDtypeStruct((1, pad, heads * GROUP * HD), BF),
        scratch_shapes=[
            pltpu.VMEM((heads, rows * GROUP, slots), F32),
            pltpu.VMEM((heads, rows * GROUP, HD), F32),
        ],
        compiler_params=pltpu.CompilerParams(vmem_limit_bytes=12 * MIB),
        cost_estimate=pl.CostEstimate(flops=1, bytes_accessed=1, transcendentals=0),
        name="attend_part",
    )(own, from_core, from_left, from_right, inv, cos, sin, lens, keys, values)


def out_kernel(has_prior, *refs):
    outs, a_ref = refs[-3:-1], refs[-1]
    priors = refs[-5:-3] if has_prior else (None, None)
    blocks = refs[: -7 if has_prior else -5]
    weights = refs[len(blocks) : len(blocks) + 2]
    pad = blocks[0].shape[1]
    for b, block in enumerate(blocks):
        a_ref[b * pad : (b + 1) * pad] = block[0].astype(F32)
    left = a_ref[...].astype(BF)
    for w_ref, prior_ref, out_ref in zip(weights, priors, outs):
        prod = jnp.dot(left, w_ref[...], preferred_element_type=F32)
        out_ref[...] = prod + prior_ref[...] if has_prior else prod


def project_out(pad, blocks, weights, prior):
    count = len(blocks)
    depth, cols = weights[0].shape
    vmem = pl.BlockSpec(memory_space=pltpu.VMEM)
    args = [*blocks, *weights] + ([] if prior is None else list(prior))
    return pl.pallas_call(
        functools.partial(out_kernel, prior is not None),
        in_specs=[vmem] * len(args),
        out_specs=[vmem] * 2,
        scratch_shapes=[pltpu.VMEM((count * pad, depth), F32)],
        out_shape=[jax.ShapeDtypeStruct((count * pad, cols), F32)] * 2,
        compiler_params=pltpu.CompilerParams(vmem_limit_bytes=12 * MIB),
        cost_estimate=pl.CostEstimate(flops=1, bytes_accessed=1, transcendentals=0),
        name="out_part",
    )(*args)


def finish_kernel(order, rows, pad, x_ref, mine_ref, other_ref, out_ref):
    pick = picker(order, gathered_slots(len(order)), rows, pad, x_ref.shape[0])
    features = jnp.dot(pick, x_ref[...], preferred_element_type=F32)
    result = (features + jnp.concatenate([mine_ref[...], other_ref[...]], axis=0)).astype(BF)
    out_ref[...] = lax.dot_general(pick, result, (((0,), (0,)), ((), ())), preferred_element_type=F32).astype(BF)


def finish(order, rows, pad, x, mine, other):
    vmem = pl.BlockSpec(memory_space=pltpu.VMEM)
    return pl.pallas_call(
        functools.partial(finish_kernel, order, rows, pad),
        in_specs=[vmem] * 3,
        out_specs=vmem,
        out_shape=jax.ShapeDtypeStruct(x.shape, BF),
        compiler_params=pltpu.CompilerParams(vmem_limit_bytes=16 * MIB),
        cost_estimate=pl.CostEstimate(flops=1, bytes_accessed=1, transcendentals=0),
        name="finish",
    )(x, mine, other)


def wide(a):
    return a.astype(F32)


def issue_order(steps):
    names = ["P0", "P1"] + ["R0", "R1"] * steps
    names += ["T0", "G0", "T1", "G1"] + ["G0", "G1"] * (steps - 2) + ["G0", "L0", "G1", "O0", "L1", "O1"]
    return names


def per_device(order, hidden_in, norm_gain, w_qkv, w_out, cache_keys, cache_values, lengths):
    rows = cache_keys.shape[0]
    pad = -(-rows // 8) * 8
    chips = len(order)
    up_pairs = [(order[p] * 2 + c, order[(p + 1) % chips] * 2 + c) for p in range(chips) for c in range(2)]
    down_pairs = [(b, a) for a, b in up_pairs]
    sibling = [(i, i ^ 1) for i in range(2 * chips)]
    before = [None]

    def after(a, *others):
        return lax.optimization_barrier((a,) + others)[0]

    def ring(sent):
        before[0] = tuple(sent.values())
        return {way: lax.ppermute(a, "gx", up_pairs if way == "up" else down_pairs) for way, a in sent.items()}

    def tied(a):
        return after(a, before[0])

    def cross(a):
        return lax.ppermute(a, "gx", sibling)

    angles = HD // 2
    inverse = 500000.0 ** (-(jnp.arange(angles, dtype=F32) * 2.0 / HD))
    angle = jnp.pad(lengths, (0, pad - rows)).astype(F32)[:, None] * inverse[None, :]
    cos = jnp.cos(angle)
    sin = jnp.sin(angle)
    cos = jnp.concatenate([cos, cos], axis=1)
    sin = jnp.concatenate([-sin, sin], axis=1)
    lens = jnp.repeat(lengths, GROUP)[:, None]

    gain = norm_gain[None, :]
    inv, w_other, caches, sums = [None], [None], [None], [None]

    def part_steps(index):
        part = PARTS[index]
        ways = dict(zip(("up", "down"), hops(index, chips)))
        steps = max(ways.values())
        sign = {"up": 1, "down": -1}
        ks = [k for k, w in sent_slots(index, chips) if w == 0]
        x = hidden_in if index == 0 else tied(hidden_in)
        keep, first, rest = project(order, index, rows, pad, x, gain, w_qkv)
        before[0] = keep
        got_first = cross(first)
        got_rest = cross(rest)
        yield

        def piece(k):
            at = ks.index(k % chips)
            return keep[at : at + 1], got_first[at : at + 1] if at < 2 else got_rest[at - 2 : at - 1]

        moved = {}
        for step in range(steps):
            sent = {}
            for way, far in ways.items():
                if step < far:
                    here, there = piece(sign[way] * (far - step))
                    total = wide(here) + wide(there)
                    sent[way] = (total + wide(tied(moved[way])) if step else wide(tied(here)) + wide(there)).astype(BF)
            moved = {**moved, **ring(sent)}
            if index == len(PARTS) - 1 and step == 0:
                w_other[0] = cross(tied(w_out))
            if index == len(PARTS) - 1 and step == 1:
                caches[0] = load("load_caches", 40, tied((cache_keys, cache_values)))
                before[0] = caches[0]
            yield
        own, from_core = piece(0)
        if index == 0:
            lanes = slice((GROUP + 2) * part[1] * HD, None)
            parts = [own, from_core, moved["up"], moved["down"]]
            square = jnp.sum(sum(wide(a[0, :, lanes]) for a in parts), axis=1)
            inv[0] = jnp.broadcast_to(lax.rsqrt(square / D + 1e-05)[:, None], (pad, HD))
        own = tied(own)
        if index == len(PARTS) - 1:
            own = after(own, w_other[0])
        attended = attend(part, rows, pad, own, from_core, moved["up"], moved["down"], inv[0], cos, sin, lens, *caches[0])
        before[0] = attended
        yield
        blocks = {0: attended}
        for step in range(steps):
            sent = {way: tied(blocks[-sign[way] * step % chips]) for way, far in ways.items() if step < far}
            for way, a in ring(sent).items():
                blocks[-sign[way] * (step + 1) % chips] = a
            yield
        weights = load("load_weights", 40, (tied(w_out), w_other[0]), part[0] * GROUP * HD, part[1] * GROUP * HD)
        yield
        sums[0] = project_out(pad, [blocks[k] for k in range(chips)], weights, sums[0])
        if index < len(PARTS) - 1:
            before[0] = sums[0]
        yield

    running = [part_steps(i) for i in range(len(PARTS))]
    for name in issue_order(chips // 2):
        next(running[int(name[-1])])
    mine, theirs = sums[0]
    return finish(order, rows, pad, hidden_in, mine, cross(theirs))


def solution(mesh):
    in_specs = (
        P("groups", "gx"),
        P("gx"),
        P("gx", None),
        P(None, "gx"),
        P(("groups", "gx"), None, None),
        P(("groups", "gx"), None, None),
        P(("groups", "gx")),
    )
    out_specs = P("groups", "gx")
    return jax.shard_map(
        functools.partial(per_device, chip_cycle(mesh)), mesh=mesh, in_specs=in_specs, out_specs=out_specs, check_vma=False
    )
```

```python
import functools

import jax
import jax.numpy as jnp
import numpy as np
from jax import lax
from jax.experimental import pallas as pl
from jax.experimental.pallas import tpu as pltpu
from jax.sharding import PartitionSpec as P

D = 8192
HEADS = 64
KVH = 8
HD = 128
GROUP = HEADS // KVH
PARTS = ((0, 4), (4, 4))
LOADS_AHEAD = 6
PIECE_GROUPS = (1, 2, 3, 4)
CUTS = 2
MIB = 1 << 20
BF = jnp.bfloat16
F32 = jnp.float32
TOKEN = jax.ShapeDtypeStruct((8, 128), jnp.float32)


def chip_cycle(mesh):
    devices = np.moveaxis(mesh.devices, mesh.axis_names.index("gx"), -1)
    devices = devices.reshape(-1, devices.shape[-1])[0][::2]
    count = len(devices)
    places = [getattr(d, "coords", None) for d in devices]
    if any(p is None for p in places):
        return list(range(count))

    def linked(a, b):
        return sum(abs(int(u) - int(v)) for u, v in zip(places[a], places[b])) == 1

    def extend(path):
        if len(path) == count:
            return path if linked(path[-1], path[0]) else None
        for nxt in range(count):
            if nxt not in path and linked(path[-1], nxt):
                found = extend(path + [nxt])
                if found:
                    return found
        return None

    return extend([0]) or list(range(count))


def hops(index, chips):
    far = chips // 2
    near = chips - 1 - far
    return (far, near) if index % 2 == 0 else (near, far)


def sent_slots(index, chips):
    up, down = hops(index, chips)
    first = [up, chips - down]
    ks = first + [k for k in range(chips) if k not in first]
    return [(k, 0) for k in ks] + [(k, 1) for k in ks]


def gathered_slots(chips):
    return [(k, w) for w in (0, 1) for k in range(chips)]


def slot_devices(order, slots):
    chips = len(order)
    me = lax.axis_index("gx")
    chip, core = me // 2, me % 2
    place = sum(jnp.where(chip == c, p, 0) for p, c in enumerate(order))

    def chip_at(distance):
        at = (place + distance) % chips
        return sum(jnp.where(at == p, c, 0) for p, c in enumerate(order))

    at = {m: chip_at(m) for m in sorted({m for m, _ in slots})}
    return [at[m] * 2 + jnp.where(core == w, 0, 1) for m, w in slots]


def picker(order, slots, rows, pad, total):
    row = lax.broadcasted_iota(jnp.int32, (pad, total), 0)
    col = lax.broadcasted_iota(jnp.int32, (pad, total), 1)
    picks = [jnp.where((col == row + dev * rows) & (row < rows), 1.0, 0.0) for dev in slot_devices(order, slots)]
    return jnp.concatenate(picks, axis=0).astype(BF)


def qkv_kernel(order, index, rows, pad, x_ref, gain_ref, w_ref, *refs):
    out_refs, (token, xs_ref, w_buf, in_sem) = refs[:4], refs[4:]
    token[...] = jnp.zeros_like(token)
    total, depth = x_ref.shape
    begin, heads = PARTS[index]
    piece = heads * HD
    pieces = GROUP + 2
    firsts = [begin * GROUP * HD + j * piece for j in range(GROUP)]
    firsts += [(HEADS + begin) * HD, (HEADS + KVH + begin) * HD]
    slots = sent_slots(index, len(order))
    def load(j):
        lanes = pl.ds(j * piece, piece)
        return pltpu.make_async_copy(w_ref.at[:, pl.ds(firsts[j], piece)], w_buf.at[:, lanes], in_sem.at[j])

    where = [(ref, at) for ref in out_refs for at in range(ref.shape[0])]

    def write(slot, lanes, value):
        ref, at = where[slot]
        ref[at, :, lanes] = value

    for j in range(LOADS_AHEAD):
        load(j).start()
    features = jnp.dot(picker(order, slots, rows, pad, total), x_ref[...], preferred_element_type=F32)
    xs_ref[...] = (features * gain_ref[...]).astype(BF)
    width = pieces * piece
    extra = out_refs[0].shape[2] - width
    if extra:
        me = lax.axis_index("gx")
        square = jnp.sum(features * features, axis=1, keepdims=True)
        lane = lax.broadcasted_iota(jnp.int32, (len(slots) * pad, extra), 1)
        high = square.astype(BF).astype(F32)
        mid = (square - high).astype(BF).astype(F32)
        low = square - high - mid
        held = jnp.where(lane == 3 * me, high, 0.0) + jnp.where(lane == 3 * me + 1, mid, 0.0) + jnp.where(lane == 3 * me + 2, low, 0.0)
        for slot in range(len(slots)):
            write(slot, slice(width, None), held[slot * pad : (slot + 1) * pad].astype(BF))
    done = 0
    for group in PIECE_GROUPS:
        for j in range(done, done + group):
            if j + LOADS_AHEAD < pieces:
                load(j + LOADS_AHEAD).start()
            load(j).wait()
        lanes = slice(done * piece, (done + group) * piece)
        out = jnp.dot(xs_ref[...], w_buf[:, lanes], preferred_element_type=F32)
        for slot in range(len(slots)):
            write(slot, lanes, out[slot * pad : (slot + 1) * pad].astype(BF))
        done += group


def project(order, index, rows, pad, x, gain, w):
    piece = PARTS[index][1] * HD
    pieces = GROUP + 2
    depth = x.shape[1]
    chips = len(order)
    extra = -(-6 * chips // 128) * 128 if index == 0 else 0
    width = pieces * piece + extra
    vmem = pl.BlockSpec(memory_space=pltpu.VMEM)
    return pl.pallas_call(
        functools.partial(qkv_kernel, order, index, rows, pad),
        in_specs=[vmem, vmem, pl.BlockSpec(memory_space=pltpu.HBM)],
        out_specs=[vmem] * 5,
        scratch_shapes=[
            pltpu.VMEM((2 * chips * pad, depth), BF),
            pltpu.VMEM((depth, pieces * piece), BF),
            pltpu.SemaphoreType.DMA((pieces,)),
        ],
        out_shape=[jax.ShapeDtypeStruct((n, pad, width), BF) for n in (2, chips - 2, 2, chips - 2)] + [TOKEN],
        compiler_params=pltpu.CompilerParams(vmem_limit_bytes=51 * MIB),
        cost_estimate=pl.CostEstimate(flops=1, bytes_accessed=1, transcendentals=0),
        name="qkv_part",
    )(x, gain, w)


def attend_kernel(part, rows, pad, own_ref, left_ref, right_ref, inv_ref, cos_ref, sin_ref, len_ref, k_ref, v_ref, out_ref, s_ref, m_ref, k_buf, v_buf, sems):
    begin, heads = part
    live = rows * GROUP
    full = pad * GROUP
    slots = k_ref.shape[1]
    scale = 1.0 / HD**0.5
    cuts = [rows * i // CUTS for i in range(CUTS + 1)]

    def load(i, which):
        source, target = ((k_ref, k_buf), (v_ref, v_buf))[which]
        seqs = pl.ds(cuts[i], cuts[i + 1] - cuts[i])
        lanes = pl.ds(begin * HD, heads * HD)
        return pltpu.make_async_copy(source.at[seqs, :, lanes], target.at[seqs], sems.at[2 * i + which])

    for which in range(2):
        for i in range(CUTS):
            load(i, which).start()
    inv = inv_ref[...]
    cos = cos_ref[...]
    sin = sin_ref[...]

    def tile(t):
        lanes = slice(t * HD, (t + 1) * HD)
        got = own_ref[0, :, lanes].astype(F32)
        return (got + (left_ref[0, :, lanes].astype(F32) + right_ref[0, :, lanes].astype(F32))) * inv

    def turned(t):
        a = tile(t)
        return (a * cos + pltpu.roll(a, HD // 2, 1) * sin).astype(BF)

    r = lax.broadcasted_iota(jnp.int32, (full, full), 0)
    c = lax.broadcasted_iota(jnp.int32, (full, full), 1)
    by_seq = jnp.where(c == (r % GROUP) * pad + r // GROUP, 1.0, 0.0).astype(BF)
    by_head = jnp.where(r == (c % GROUP) * pad + c // GROUP, 1.0, 0.0).astype(BF)
    r2 = lax.broadcasted_iota(jnp.int32, (full, pad), 0)
    c2 = lax.broadcasted_iota(jnp.int32, (full, pad), 1)
    spread = jnp.where(c2 == r2 // GROUP, 1.0, 0.0).astype(BF)
    valid = lax.broadcasted_iota(jnp.int32, (live, slots), 1) < len_ref[...]

    queries, owns, values_new = [], [], []
    for kk in range(heads):
        q = jnp.concatenate([turned(kk * GROUP + g).astype(F32) for g in range(GROUP)], axis=0).astype(BF)
        q = jnp.dot(by_seq, q, preferred_element_type=F32)
        k_new = jnp.dot(spread, turned(heads * GROUP + kk), preferred_element_type=F32)
        values_new.append(jnp.dot(spread, tile(heads * GROUP + heads + kk).astype(BF), preferred_element_type=F32)[:live])
        owns.append((jnp.sum(q * k_new, axis=1, keepdims=True) * scale)[:live])
        queries.append(q)
    for i in range(CUTS):
        load(i, 0).wait()
        for kk in range(heads):
            for s in range(cuts[i], cuts[i + 1]):
                s_ref[kk, s * GROUP : (s + 1) * GROUP] = lax.dot_general(
                    queries[kk][s * GROUP : (s + 1) * GROUP].astype(BF),
                    k_buf[s, :, kk * HD : (kk + 1) * HD],
                    (((1,), (1,)), ((), ())),
                    preferred_element_type=F32,
                )
    own_weights = []
    for kk in range(heads):
        scores = jnp.where(valid, s_ref[kk] * scale, -1e30)
        top = jnp.maximum(jnp.max(scores, axis=1, keepdims=True), owns[kk])
        expo = jnp.where(valid, jnp.exp(scores - top), 0.0)
        own_expo = jnp.exp(owns[kk] - top)
        total = jnp.sum(expo, axis=1, keepdims=True) + own_expo
        s_ref[kk] = expo / total
        own_weights.append((own_expo / total).astype(BF).astype(F32))
    for i in range(CUTS):
        load(i, 1).wait()
        for kk in range(heads):
            for s in range(cuts[i], cuts[i + 1]):
                m_ref[kk, s * GROUP : (s + 1) * GROUP] = jnp.dot(
                    s_ref[kk, s * GROUP : (s + 1) * GROUP].astype(BF),
                    v_buf[s, :, kk * HD : (kk + 1) * HD],
                    preferred_element_type=F32,
                )
    for kk in range(heads):
        mixed = m_ref[kk] + own_weights[kk] * values_new[kk]
        mixed = jnp.concatenate([mixed, jnp.zeros((full - live, HD), F32)], axis=0).astype(BF)
        mixed = jnp.dot(by_head, mixed, preferred_element_type=F32)
        for g in range(GROUP):
            out_ref[0, :, (kk * GROUP + g) * HD : (kk * GROUP + g + 1) * HD] = mixed[g * pad : (g + 1) * pad].astype(BF)


def load(name, limit, arrays, begin=0, count=None):
    count = arrays[0].shape[0] if count is None else count

    def kernel(*refs):
        token, sems = refs[-2:]
        copies = [
            pltpu.make_async_copy(refs[i].at[pl.ds(begin, count)], refs[len(arrays) + i], sems.at[i]) for i in range(len(arrays))
        ]
        for copy in copies:
            copy.start()
        for copy in copies:
            copy.wait()
        token[...] = jnp.zeros_like(token)

    *held, token = pl.pallas_call(
        kernel,
        in_specs=[pl.BlockSpec(memory_space=pltpu.HBM)] * len(arrays),
        out_specs=[pl.BlockSpec(memory_space=pltpu.VMEM)] * (len(arrays) + 1),
        out_shape=[jax.ShapeDtypeStruct((count,) + a.shape[1:], BF) for a in arrays] + [TOKEN],
        scratch_shapes=[pltpu.SemaphoreType.DMA((len(arrays),))],
        compiler_params=pltpu.CompilerParams(vmem_limit_bytes=limit * MIB),
        cost_estimate=pl.CostEstimate(flops=1, bytes_accessed=1, transcendentals=0),
        name=name,
    )(*arrays)
    return held, token


def attend(part, rows, pad, own, from_left, from_right, inv, cos, sin, lens, keys, values):
    slots = keys.shape[1]
    heads = part[1]
    vmem = pl.BlockSpec(memory_space=pltpu.VMEM)
    return pl.pallas_call(
        functools.partial(attend_kernel, part, rows, pad),
        in_specs=[vmem] * 7 + [pl.BlockSpec(memory_space=pltpu.HBM)] * 2,
        out_specs=vmem,
        out_shape=jax.ShapeDtypeStruct((1, pad, heads * GROUP * HD), BF),
        scratch_shapes=[
            pltpu.VMEM((heads, rows * GROUP, slots), F32),
            pltpu.VMEM((heads, rows * GROUP, HD), F32),
            pltpu.VMEM((rows, slots, heads * HD), BF),
            pltpu.VMEM((rows, slots, heads * HD), BF),
            pltpu.SemaphoreType.DMA((2 * CUTS,)),
        ],
        compiler_params=pltpu.CompilerParams(vmem_limit_bytes=51 * MIB),
        cost_estimate=pl.CostEstimate(flops=1, bytes_accessed=1, transcendentals=0),
        name="attend_part",
    )(own, from_left, from_right, inv, cos, sin, lens, keys, values)


def out_kernel(has_prior, *refs):
    outs, a_ref = refs[-3:-1], refs[-1]
    priors = refs[-5:-3] if has_prior else (None, None)
    blocks = refs[: -7 if has_prior else -5]
    weights = refs[len(blocks) : len(blocks) + 2]
    pad = blocks[0].shape[1]
    for b, block in enumerate(blocks):
        a_ref[b * pad : (b + 1) * pad] = block[0].astype(F32)
    left = a_ref[...].astype(BF)
    for w_ref, prior_ref, out_ref in zip(weights, priors, outs):
        prod = jnp.dot(left, w_ref[...], preferred_element_type=F32)
        out_ref[...] = prod + prior_ref[...] if has_prior else prod


def project_out(pad, blocks, weights, prior):
    count = len(blocks)
    depth, cols = weights[0].shape
    vmem = pl.BlockSpec(memory_space=pltpu.VMEM)
    args = [*blocks, *weights] + ([] if prior is None else list(prior))
    return pl.pallas_call(
        functools.partial(out_kernel, prior is not None),
        in_specs=[vmem] * len(args),
        out_specs=[vmem] * 2,
        scratch_shapes=[pltpu.VMEM((count * pad, depth), F32)],
        out_shape=[jax.ShapeDtypeStruct((count * pad, cols), F32)] * 2,
        compiler_params=pltpu.CompilerParams(vmem_limit_bytes=12 * MIB),
        cost_estimate=pl.CostEstimate(flops=1, bytes_accessed=1, transcendentals=0),
        name="out_part",
    )(*args)


def finish_kernel(order, rows, pad, x_ref, mine_ref, other_ref, out_ref):
    pick = picker(order, gathered_slots(len(order)), rows, pad, x_ref.shape[0])
    features = jnp.dot(pick, x_ref[...], preferred_element_type=F32)
    result = (features + jnp.concatenate([mine_ref[...], other_ref[...]], axis=0)).astype(BF)
    out_ref[...] = lax.dot_general(pick, result, (((0,), (0,)), ((), ())), preferred_element_type=F32).astype(BF)


def finish(order, rows, pad, x, mine, other):
    vmem = pl.BlockSpec(memory_space=pltpu.VMEM)
    return pl.pallas_call(
        functools.partial(finish_kernel, order, rows, pad),
        in_specs=[vmem] * 3,
        out_specs=vmem,
        out_shape=jax.ShapeDtypeStruct(x.shape, BF),
        compiler_params=pltpu.CompilerParams(vmem_limit_bytes=16 * MIB),
        cost_estimate=pl.CostEstimate(flops=1, bytes_accessed=1, transcendentals=0),
        name="finish",
    )(x, mine, other)


def wide(a):
    return a.astype(F32)


def issue_order(steps):
    names = ["P0", "R0", "P1", "R0", "R1"] + ["R0", "R1"] * (steps - 2) + ["R1"]
    names += ["T0", "G0", "T1", "G1", "L0", "G0", "G1", "L1"] + ["G0", "G1"] * (steps - 2) + ["O0", "O1"]
    return names


def per_device(order, hidden_in, norm_gain, w_qkv, w_out, cache_keys, cache_values, lengths):
    rows = cache_keys.shape[0]
    pad = -(-rows // 8) * 8
    chips = len(order)
    up_pairs = [(order[p] * 2 + c, order[(p + 1) % chips] * 2 + c) for p in range(chips) for c in range(2)]
    down_pairs = [(b, a) for a, b in up_pairs]
    sibling = [(i, i ^ 1) for i in range(2 * chips)]
    before = [None]

    def after(a, *others):
        return lax.optimization_barrier((a,) + others)[0]

    def ring(sent):
        before[0] = tuple(sent.values())
        return {way: lax.ppermute(a, "gx", up_pairs if way == "up" else down_pairs) for way, a in sent.items()}

    def tied(a):
        return after(a, before[0])

    def cross(a):
        return lax.ppermute(a, "gx", sibling)

    def positions(lengths):
        angles = HD // 2
        inverse = 500000.0 ** (-(jnp.arange(angles, dtype=F32) * 2.0 / HD))
        angle = jnp.pad(lengths, (0, pad - rows)).astype(F32)[:, None] * inverse[None, :]
        cos = jnp.cos(angle)
        sin = jnp.sin(angle)
        return jnp.concatenate([cos, cos], axis=1), jnp.concatenate([-sin, sin], axis=1), jnp.repeat(lengths, GROUP)[:, None]

    gain = norm_gain[None, :]
    inv, w_other, places, sums = [None], [None], [None], [None]

    def part_steps(index):
        part = PARTS[index]
        ways = dict(zip(("up", "down"), hops(index, chips)))
        steps = max(ways.values())
        sign = {"up": 1, "down": -1}
        ks = [k for k, w in sent_slots(index, chips) if w == 0]
        x = hidden_in if index == 0 else tied(hidden_in)
        keep_first, keep_rest, first, rest, before[0] = project(order, index, rows, pad, x, gain, w_qkv)
        got_first = cross(first)
        got_rest = cross(rest)
        yield

        front = (wide(tied(keep_first)) + wide(got_first)).astype(BF)
        back = []

        def piece(k):
            at = ks.index(k % chips)
            if at < 2:
                return front[at : at + 1]
            if not back:
                back.append((wide(keep_rest) + wide(got_rest)).astype(BF))
            return back[0][at - 2 : at - 1]

        moved = {}
        for step in range(steps):
            sent = {}
            for way, far in ways.items():
                if step < far:
                    sent[way] = piece(sign[way] * (far - step))
                    if step:
                        sent[way] = (wide(sent[way]) + wide(tied(moved[way]))).astype(BF)
            moved = {**moved, **ring(sent)}
            if index == 1 and step == 0:
                w_other[0] = cross(tied(w_out))
            if index == 1 and step == 1:
                places[0] = positions(tied(lengths))
            yield
        own = piece(0)
        if index == 0:
            lanes = slice((GROUP + 2) * part[1] * HD, None)
            parts = [own, moved["up"], moved["down"]]
            square = jnp.sum(sum(wide(a[0, :, lanes]) for a in parts), axis=1)
            inv[0] = jnp.broadcast_to(lax.rsqrt(square / D + 1e-05)[:, None], (pad, HD))
        own = tied(own)
        if index == 1:
            own = after(own, w_other[0])
        attended = attend(part, rows, pad, own, moved["up"], moved["down"], inv[0], *places[0], cache_keys, cache_values)
        before[0] = attended
        yield
        blocks = {0: attended}
        for step in range(steps):
            sent = {way: tied(blocks[-sign[way] * step % chips]) for way, far in ways.items() if step < far}
            for way, a in ring(sent).items():
                blocks[-sign[way] * (step + 1) % chips] = a
            yield
            if step == index:
                held = (tied(w_out), w_other[0])
                weights, before[0] = load("load_weights", 40, held, part[0] * GROUP * HD, part[1] * GROUP * HD)
                yield
        sums[0] = project_out(pad, [blocks[k] for k in range(chips)], weights, sums[0])
        if index < len(PARTS) - 1:
            before[0] = sums[0]
        yield

    running = [part_steps(i) for i in range(len(PARTS))]
    for name in issue_order(chips // 2):
        next(running[int(name[-1])])
    mine, theirs = sums[0]
    return finish(order, rows, pad, hidden_in, mine, cross(theirs))


def solution(mesh):
    in_specs = (
        P("groups", "gx"),
        P("gx"),
        P("gx", None),
        P(None, "gx"),
        P(("groups", "gx"), None, None),
        P(("groups", "gx"), None, None),
        P(("groups", "gx")),
    )
    out_specs = P("groups", "gx")
    return jax.shard_map(
        functools.partial(per_device, chip_cycle(mesh)), mesh=mesh, in_specs=in_specs, out_specs=out_specs, check_vma=False
    )
```

```python
import functools

import jax
import jax.numpy as jnp
import numpy as np
from jax import lax
from jax.experimental import pallas as pl
from jax.experimental.pallas import tpu as pltpu
from jax.sharding import PartitionSpec as P

D = 8192
HEADS = 64
KVH = 8
HD = 128
GROUP = HEADS // KVH
PARTS = ((0, 4), (4, 4))
LOADS_AHEAD = 6
PIECE_GROUPS = (1, 2, 3, 4)
CUTS = 2
MIB = 1 << 20
BF = jnp.bfloat16
F32 = jnp.float32
TOKEN = jax.ShapeDtypeStruct((8, 128), jnp.float32)


def chip_cycle(mesh):
    devices = np.moveaxis(mesh.devices, mesh.axis_names.index("gx"), -1)
    devices = devices.reshape(-1, devices.shape[-1])[0][::2]
    count = len(devices)
    places = [getattr(d, "coords", None) for d in devices]
    if any(p is None for p in places):
        return list(range(count))

    def linked(a, b):
        return sum(abs(int(u) - int(v)) for u, v in zip(places[a], places[b])) == 1

    def extend(path):
        if len(path) == count:
            return path if linked(path[-1], path[0]) else None
        for nxt in range(count):
            if nxt not in path and linked(path[-1], nxt):
                found = extend(path + [nxt])
                if found:
                    return found
        return None

    return extend([0]) or list(range(count))


def hops(index, chips):
    far = chips // 2
    near = chips - 1 - far
    return (far, near) if index % 2 == 0 else (near, far)


def sent_slots(index, chips):
    up, down = hops(index, chips)
    first = [up, chips - down]
    ks = first + [k for k in range(chips) if k not in first]
    return [(k, 0) for k in ks] + [(k, 1) for k in ks]


def gathered_slots(chips):
    return [(k, w) for w in (0, 1) for k in range(chips)]


def split_rows(rows):
    assert rows % 8 == 6
    return rows // 8


def packed_width(rows, width):
    return split_rows(rows) * width + 3 * width // 4


def pack_rest(a):
    row = lax.broadcasted_iota(jnp.int32, (8, HD), 0)
    b, c, d = pltpu.roll(a[1], 6, 0), pltpu.roll(a[2], 4, 0), pltpu.roll(a[3], 2, 0)
    return a[0] + jnp.where(row >= 6, b, 0.0), jnp.where(row < 4, b, c), jnp.where(row < 2, c, d)


def unpack_rest(tiles, q):
    row = lax.broadcasted_iota(jnp.int32, (8, HD), 0)
    first, second, third = tiles
    if q == 0:
        return jnp.where(row < 6, first, 0.0)
    if q == 1:
        return pltpu.roll(jnp.where(row >= 6, first, jnp.where(row < 4, second, 0.0)), 2, 0)
    if q == 2:
        return pltpu.roll(jnp.where(row >= 4, second, jnp.where(row < 2, third, 0.0)), 4, 0)
    return pltpu.roll(jnp.where(row >= 2, third, 0.0), 6, 0)


def pack_tiles(rows, width, lane, tiles, write):
    full = split_rows(rows)
    for i in range(full):
        for q in range(4):
            write(i * width + lane + q * HD, tiles[q][i * 8 : (i + 1) * 8])
    for i, rest in enumerate(pack_rest([a[full * 8 : full * 8 + 8] for a in tiles])):
        write(full * width + lane * 3 // 4 + i * HD, rest)


def unpack_tile(rows, width, lane, read):
    full = split_rows(rows)
    group, q = lane // (4 * HD) * 4 * HD, lane // HD % 4
    rest = [read(full * width + group * 3 // 4 + i * HD) for i in range(3)]
    return jnp.concatenate([read(i * width + lane) for i in range(full)] + [unpack_rest(rest, q)], axis=0)


def slot_devices(order, slots):
    chips = len(order)
    me = lax.axis_index("gx")
    chip, core = me // 2, me % 2
    place = sum(jnp.where(chip == c, p, 0) for p, c in enumerate(order))

    def chip_at(distance):
        at = (place + distance) % chips
        return sum(jnp.where(at == p, c, 0) for p, c in enumerate(order))

    at = {m: chip_at(m) for m in sorted({m for m, _ in slots})}
    return [at[m] * 2 + jnp.where(core == w, 0, 1) for m, w in slots]


def picker(order, slots, rows, pad, total):
    row = lax.broadcasted_iota(jnp.int32, (pad, total), 0)
    col = lax.broadcasted_iota(jnp.int32, (pad, total), 1)
    picks = [jnp.where((col == row + dev * rows) & (row < rows), 1.0, 0.0) for dev in slot_devices(order, slots)]
    return jnp.concatenate(picks, axis=0).astype(BF)


def qkv_kernel(order, index, rows, pad, x_ref, gain_ref, w_ref, *refs):
    out_refs, (token, xs_ref, x_buf, gain_buf, w_buf, in_sem) = refs[:4], refs[4:]
    token[...] = jnp.zeros_like(token)
    total, depth = x_ref.shape
    begin, heads = PARTS[index]
    piece = heads * HD
    pieces = GROUP + 2
    firsts = [begin * GROUP * HD + j * piece for j in range(GROUP)]
    firsts += [(HEADS + begin) * HD, (HEADS + KVH + begin) * HD]
    slots = sent_slots(index, len(order))
    def load(j):
        lanes = pl.ds(j * piece, piece)
        return pltpu.make_async_copy(w_ref.at[:, pl.ds(firsts[j], piece)], w_buf.at[:, lanes], in_sem.at[j])

    where = [(ref, at) for ref in out_refs for at in range(ref.shape[0])]

    def write(slot, lane, value):
        ref, at = where[slot]
        ref[at, :, lane : lane + HD] = value.astype(BF)

    small = [
        pltpu.make_async_copy(x_ref, x_buf, in_sem.at[pieces]),
        pltpu.make_async_copy(gain_ref, gain_buf, in_sem.at[pieces + 1]),
    ]
    for copy in small:
        copy.start()
    for j in range(LOADS_AHEAD):
        load(j).start()
    pick = picker(order, slots, rows, pad, total)
    for copy in small:
        copy.wait()
    features = jnp.dot(pick, x_buf[...], preferred_element_type=F32)
    xs_ref[...] = (features * gain_buf[...]).astype(BF)
    width = pieces * piece
    packed = packed_width(rows, width)
    extra = (out_refs[0].shape[2] - packed) // 3
    if extra:
        me = lax.axis_index("gx")
        square = jnp.sum(features * features, axis=1, keepdims=True)
        lane = lax.broadcasted_iota(jnp.int32, (len(slots) * pad, extra), 1)
        high = square.astype(BF).astype(F32)
        mid = (square - high).astype(BF).astype(F32)
        low = square - high - mid
        held = jnp.where(lane == 3 * me, high, 0.0) + jnp.where(lane == 3 * me + 1, mid, 0.0) + jnp.where(lane == 3 * me + 2, low, 0.0)
        for slot in range(len(slots)):
            for i in range(3):
                write(slot, packed + i * extra, held[slot * pad + i * 8 : slot * pad + i * 8 + 8])
    done = 0
    for group in PIECE_GROUPS:
        for j in range(done, done + group):
            if j + LOADS_AHEAD < pieces:
                load(j + LOADS_AHEAD).start()
            load(j).wait()
        lanes = slice(done * piece, (done + group) * piece)
        out = jnp.dot(xs_ref[...], w_buf[:, lanes], preferred_element_type=F32)
        for slot in range(len(slots)):
            block = out[slot * pad : (slot + 1) * pad]
            for lane in range(0, group * piece, 4 * HD):
                tiles = [block[:, lane + q * HD : lane + (q + 1) * HD] for q in range(4)]
                pack_tiles(rows, width, done * piece + lane, tiles, functools.partial(write, slot))
        done += group


def project(order, index, rows, pad, x, gain, w):
    piece = PARTS[index][1] * HD
    pieces = GROUP + 2
    depth = x.shape[1]
    chips = len(order)
    extra = -(-6 * chips // 128) * 128 if index == 0 else 0
    width = packed_width(rows, pieces * piece) + 3 * extra
    vmem = pl.BlockSpec(memory_space=pltpu.VMEM)
    return pl.pallas_call(
        functools.partial(qkv_kernel, order, index, rows, pad),
        in_specs=[pl.BlockSpec(memory_space=pltpu.HBM)] * 3,
        out_specs=[vmem] * 5,
        scratch_shapes=[
            pltpu.VMEM((2 * chips * pad, depth), BF),
            pltpu.VMEM(x.shape, BF),
            pltpu.VMEM(gain.shape, F32),
            pltpu.VMEM((depth, pieces * piece), BF),
            pltpu.SemaphoreType.DMA((pieces + 2,)),
        ],
        out_shape=[jax.ShapeDtypeStruct((n, 8, width), BF) for n in (2, chips - 2, 2, chips - 2)] + [TOKEN],
        compiler_params=pltpu.CompilerParams(vmem_limit_bytes=51 * MIB),
        cost_estimate=pl.CostEstimate(flops=1, bytes_accessed=1, transcendentals=0),
        name="qkv_part",
    )(x, gain, w)


def attend_kernel(part, rows, pad, own_ref, left_ref, right_ref, inv_ref, cos_ref, sin_ref, len_ref, k_ref, v_ref, out_ref, s_ref, m_ref, k_buf, v_buf, sems):
    begin, heads = part
    live = rows * GROUP
    full = pad * GROUP
    slots = k_ref.shape[1]
    scale = 1.0 / HD**0.5
    cuts = [rows * i // CUTS for i in range(CUTS + 1)]

    def load(i, which):
        source, target = ((k_ref, k_buf), (v_ref, v_buf))[which]
        seqs = pl.ds(cuts[i], cuts[i + 1] - cuts[i])
        lanes = pl.ds(begin * HD, heads * HD)
        return pltpu.make_async_copy(source.at[seqs, :, lanes], target.at[seqs], sems.at[2 * i + which])

    for which in range(2):
        for i in range(CUTS):
            load(i, which).start()
    inv = inv_ref[...]
    cos = cos_ref[...]
    sin = sin_ref[...]

    def summed(lane):
        lanes = slice(lane, lane + HD)
        got = own_ref[0, :, lanes].astype(F32)
        return got + (left_ref[0, :, lanes].astype(F32) + right_ref[0, :, lanes].astype(F32))

    def tile(t):
        return unpack_tile(rows, (GROUP + 2) * heads * HD, t * HD, summed) * inv

    def turned(t):
        a = tile(t)
        return (a * cos + pltpu.roll(a, HD // 2, 1) * sin).astype(BF)

    r = lax.broadcasted_iota(jnp.int32, (full, full), 0)
    c = lax.broadcasted_iota(jnp.int32, (full, full), 1)
    by_seq = jnp.where(c == (r % GROUP) * pad + r // GROUP, 1.0, 0.0).astype(BF)
    by_head = jnp.where(r == (c % GROUP) * pad + c // GROUP, 1.0, 0.0).astype(BF)
    r2 = lax.broadcasted_iota(jnp.int32, (full, pad), 0)
    c2 = lax.broadcasted_iota(jnp.int32, (full, pad), 1)
    spread = jnp.where(c2 == r2 // GROUP, 1.0, 0.0).astype(BF)
    valid = lax.broadcasted_iota(jnp.int32, (live, slots), 1) < len_ref[...]

    def write(lane, value):
        out_ref[0, :, lane : lane + HD] = value.astype(BF)

    queries, owns, values_new = [], [], []
    for kk in range(heads):
        q = jnp.concatenate([turned(kk * GROUP + g).astype(F32) for g in range(GROUP)], axis=0).astype(BF)
        q = jnp.dot(by_seq, q, preferred_element_type=F32)
        k_new = jnp.dot(spread, turned(heads * GROUP + kk), preferred_element_type=F32)
        values_new.append(jnp.dot(spread, tile(heads * GROUP + heads + kk).astype(BF), preferred_element_type=F32)[:live])
        owns.append((jnp.sum(q * k_new, axis=1, keepdims=True) * scale)[:live])
        queries.append(q)
    for i in range(CUTS):
        load(i, 0).wait()
        for kk in range(heads):
            for s in range(cuts[i], cuts[i + 1]):
                s_ref[kk, s * GROUP : (s + 1) * GROUP] = lax.dot_general(
                    queries[kk][s * GROUP : (s + 1) * GROUP].astype(BF),
                    k_buf[s, :, kk * HD : (kk + 1) * HD],
                    (((1,), (1,)), ((), ())),
                    preferred_element_type=F32,
                )
    own_weights = []
    for kk in range(heads):
        scores = jnp.where(valid, s_ref[kk] * scale, -1e30)
        top = jnp.maximum(jnp.max(scores, axis=1, keepdims=True), owns[kk])
        expo = jnp.where(valid, jnp.exp(scores - top), 0.0)
        own_expo = jnp.exp(owns[kk] - top)
        total = jnp.sum(expo, axis=1, keepdims=True) + own_expo
        s_ref[kk] = expo / total
        own_weights.append((own_expo / total).astype(BF).astype(F32))
    for i in range(CUTS):
        load(i, 1).wait()
        for kk in range(heads):
            for s in range(cuts[i], cuts[i + 1]):
                m_ref[kk, s * GROUP : (s + 1) * GROUP] = jnp.dot(
                    s_ref[kk, s * GROUP : (s + 1) * GROUP].astype(BF),
                    v_buf[s, :, kk * HD : (kk + 1) * HD],
                    preferred_element_type=F32,
                )
    for kk in range(heads):
        mixed = m_ref[kk] + own_weights[kk] * values_new[kk]
        mixed = jnp.concatenate([mixed, jnp.zeros((full - live, HD), F32)], axis=0).astype(BF)
        mixed = jnp.dot(by_head, mixed, preferred_element_type=F32)
        tiles = [mixed[g * pad : (g + 1) * pad] for g in range(GROUP)]
        for g in range(0, GROUP, 4):
            pack_tiles(rows, heads * GROUP * HD, (kk * GROUP + g) * HD, tiles[g : g + 4], write)


def load(name, limit, arrays, begin=0, count=None):
    count = arrays[0].shape[0] if count is None else count

    def kernel(*refs):
        token, sems = refs[-2:]
        copies = [
            pltpu.make_async_copy(refs[i].at[pl.ds(begin, count)], refs[len(arrays) + i], sems.at[i]) for i in range(len(arrays))
        ]
        for copy in copies:
            copy.start()
        for copy in copies:
            copy.wait()
        token[...] = jnp.zeros_like(token)

    *held, token = pl.pallas_call(
        kernel,
        in_specs=[pl.BlockSpec(memory_space=pltpu.HBM)] * len(arrays),
        out_specs=[pl.BlockSpec(memory_space=pltpu.VMEM)] * (len(arrays) + 1),
        out_shape=[jax.ShapeDtypeStruct((count,) + a.shape[1:], BF) for a in arrays] + [TOKEN],
        scratch_shapes=[pltpu.SemaphoreType.DMA((len(arrays),))],
        compiler_params=pltpu.CompilerParams(vmem_limit_bytes=limit * MIB),
        cost_estimate=pl.CostEstimate(flops=1, bytes_accessed=1, transcendentals=0),
        name=name,
    )(*arrays)
    return held, token


def attend(part, rows, pad, own, from_left, from_right, inv, cos, sin, lens, keys, values):
    slots = keys.shape[1]
    heads = part[1]
    vmem = pl.BlockSpec(memory_space=pltpu.VMEM)
    return pl.pallas_call(
        functools.partial(attend_kernel, part, rows, pad),
        in_specs=[vmem] * 7 + [pl.BlockSpec(memory_space=pltpu.HBM)] * 2,
        out_specs=vmem,
        out_shape=jax.ShapeDtypeStruct((1, 8, packed_width(rows, heads * GROUP * HD)), BF),
        scratch_shapes=[
            pltpu.VMEM((heads, rows * GROUP, slots), F32),
            pltpu.VMEM((heads, rows * GROUP, HD), F32),
            pltpu.VMEM((rows, slots, heads * HD), BF),
            pltpu.VMEM((rows, slots, heads * HD), BF),
            pltpu.SemaphoreType.DMA((2 * CUTS,)),
        ],
        compiler_params=pltpu.CompilerParams(vmem_limit_bytes=51 * MIB),
        cost_estimate=pl.CostEstimate(flops=1, bytes_accessed=1, transcendentals=0),
        name="attend_part",
    )(own, from_left, from_right, inv, cos, sin, lens, keys, values)


def features_kernel(order, rows, pad, x_ref, x_other_ref, mine_ref, theirs_ref):
    slots = gathered_slots(len(order))
    pick = picker(order, slots[: len(order)], rows, pad, x_ref.shape[0])
    mine_ref[...] = jnp.dot(pick, x_ref[...], preferred_element_type=F32)
    theirs_ref[...] = jnp.dot(pick, x_other_ref[...], preferred_element_type=F32)


def features_of(order, rows, pad, x, x_other):
    vmem = pl.BlockSpec(memory_space=pltpu.VMEM)
    return pl.pallas_call(
        functools.partial(features_kernel, order, rows, pad),
        in_specs=[vmem] * 2,
        out_specs=[vmem] * 2,
        out_shape=[jax.ShapeDtypeStruct((len(order) * pad, x.shape[1]), F32)] * 2,
        compiler_params=pltpu.CompilerParams(vmem_limit_bytes=8 * MIB),
        cost_estimate=pl.CostEstimate(flops=1, bytes_accessed=1, transcendentals=0),
        name="features",
    )(x, x_other)


def out_kernel(rows, pad, *refs):
    outs, a_ref = refs[-3:-1], refs[-1]
    priors, weights, blocks = refs[-5:-3], refs[-7:-5], refs[:-7]
    width = weights[0].shape[0]
    for b, block in enumerate(blocks):
        for lane in range(0, width, HD):
            tile = unpack_tile(rows, width, lane, lambda at: block[0, :, at : at + HD].astype(F32))
            a_ref[b * pad : (b + 1) * pad, lane : lane + HD] = tile
    left = a_ref[...].astype(BF)
    for w_ref, prior_ref, out_ref in zip(weights, priors, outs):
        out_ref[...] = (prior_ref[...] + jnp.dot(left, w_ref[...], preferred_element_type=F32)).astype(out_ref.dtype)


def project_out(rows, pad, blocks, weights, prior, dtype):
    count = len(blocks)
    depth, cols = weights[0].shape
    vmem = pl.BlockSpec(memory_space=pltpu.VMEM)
    args = [*blocks, *weights, *prior]
    return pl.pallas_call(
        functools.partial(out_kernel, rows, pad),
        in_specs=[vmem] * len(args),
        out_specs=[vmem] * 2,
        scratch_shapes=[pltpu.VMEM((count * pad, depth), F32)],
        out_shape=[jax.ShapeDtypeStruct((count * pad, cols), dtype)] * 2,
        compiler_params=pltpu.CompilerParams(vmem_limit_bytes=12 * MIB),
        cost_estimate=pl.CostEstimate(flops=1, bytes_accessed=1, transcendentals=0),
        name="out_part",
    )(*args)


def place_kernel(order, rows, pad, which, rows_ref, *refs):
    out_ref = refs[-1]
    chips = len(order)
    pick = picker(order, gathered_slots(chips)[which * chips : (which + 1) * chips], rows, pad, out_ref.shape[0])
    placed = lax.dot_general(pick, rows_ref[...], (((0,), (0,)), ((), ())), preferred_element_type=F32)
    if len(refs) > 1:
        placed = placed + refs[0][...].astype(F32)
    out_ref[...] = placed.astype(BF)


def place(order, rows, pad, which, result, *other):
    vmem = pl.BlockSpec(memory_space=pltpu.VMEM)
    return pl.pallas_call(
        functools.partial(place_kernel, order, rows, pad, which),
        in_specs=[vmem] * (1 + len(other)),
        out_specs=vmem,
        out_shape=jax.ShapeDtypeStruct((2 * len(order) * rows, result.shape[1]), BF),
        compiler_params=pltpu.CompilerParams(vmem_limit_bytes=8 * MIB),
        cost_estimate=pl.CostEstimate(flops=1, bytes_accessed=1, transcendentals=0),
        name="place",
    )(result, *other)


def wide(a):
    return a.astype(F32)


def issue_order(steps):
    names = ["P0", "R0", "P1", "R0", "R1"] + ["R0", "R1"] * (steps - 2) + ["R1"]
    return names + ["T0", "G0", "T1", "G1", "G0", "W0", "G1", "G0", "W1", "G1"] + ["G0", "G1"] * (steps - 3) + ["O0", "O1"]


def per_device(order, hidden_in, norm_gain, w_qkv, w_out, cache_keys, cache_values, lengths):
    rows = cache_keys.shape[0]
    pad = -(-rows // 8) * 8
    chips = len(order)
    up_pairs = [(order[p] * 2 + c, order[(p + 1) % chips] * 2 + c) for p in range(chips) for c in range(2)]
    down_pairs = [(b, a) for a, b in up_pairs]
    sibling = [(i, i ^ 1) for i in range(2 * chips)]
    before = [None]

    def after(a, *others):
        return lax.optimization_barrier((a,) + others)[0]

    def ring(sent):
        before[0] = tuple(sent.values())
        return {way: lax.ppermute(a, "gx", up_pairs if way == "up" else down_pairs) for way, a in sent.items()}

    def tied(a):
        return after(a, before[0])

    def cross(a):
        return lax.ppermute(a, "gx", sibling)

    def positions(lengths):
        angles = HD // 2
        inverse = 500000.0 ** (-(jnp.arange(angles, dtype=F32) * 2.0 / HD))
        angle = jnp.pad(lengths, (0, pad - rows)).astype(F32)[:, None] * inverse[None, :]
        cos = jnp.cos(angle)
        sin = jnp.sin(angle)
        return jnp.concatenate([cos, cos], axis=1), jnp.concatenate([-sin, sin], axis=1), jnp.repeat(lengths, GROUP)[:, None]

    gain = norm_gain[None, :]
    inv, w_other, x_other, places, sums, weights = [None], [None], [None], [None], [None], {}

    def part_steps(index):
        part = PARTS[index]
        ways = dict(zip(("up", "down"), hops(index, chips)))
        steps = max(ways.values())
        sign = {"up": 1, "down": -1}
        ks = [k for k, w in sent_slots(index, chips) if w == 0]
        x = hidden_in if index == 0 else tied(hidden_in)
        keep_first, keep_rest, first, rest, before[0] = project(order, index, rows, pad, x, gain, w_qkv)
        got_first = cross(first)
        got_rest = cross(rest)
        yield

        front = (wide(tied(keep_first)) + wide(got_first)).astype(BF)
        back = []

        def piece(k):
            at = ks.index(k % chips)
            if at < 2:
                return front[at : at + 1]
            if not back:
                back.append((wide(keep_rest) + wide(got_rest)).astype(BF))
            return back[0][at - 2 : at - 1]

        moved = {}
        for step in range(steps):
            sent = {}
            for way, far in ways.items():
                if step < far:
                    sent[way] = piece(sign[way] * (far - step))
                    if step:
                        sent[way] = (wide(sent[way]) + wide(tied(moved[way]))).astype(BF)
            moved = {**moved, **ring(sent)}
            if index == 1 and step == 0:
                w_other[0] = cross(tied(w_out))
                x_other[0] = cross(tied(hidden_in))
            if index == 1 and step == 1:
                places[0] = positions(tied(lengths))
                sums[0] = features_of(order, rows, pad, hidden_in, x_other[0])
            yield
        own = piece(0)
        if index == 0:
            first = packed_width(rows, (GROUP + 2) * part[1] * HD)
            terms = sum(wide(a[0, :, first:]) for a in (own, moved["up"], moved["down"]))
            square = jnp.sum(terms.reshape(8, 3, -1), axis=2).T.reshape(pad)
            inv[0] = jnp.broadcast_to(lax.rsqrt(square / D + 1e-05)[:, None], (pad, HD))
        own = tied(own)
        if index == 0:
            own = after(own, x_other[0])
        if index == 1 and 1 not in weights:
            own = after(own, w_other[0])
        attended = attend(part, rows, pad, own, moved["up"], moved["down"], inv[0], *places[0], cache_keys, cache_values)
        before[0] = attended
        yield
        blocks = {0: attended}
        for step in range(steps):
            sent = {way: tied(blocks[-sign[way] * step % chips]) for way, far in ways.items() if step < far}
            for way, a in ring(sent).items():
                blocks[-sign[way] * (step + 1) % chips] = a
            yield
        last = index == len(PARTS) - 1
        sums[0] = project_out(rows, pad, [blocks[k] for k in range(chips)], weights[index], sums[0], BF if last else F32)
        yield

    running = [part_steps(i) for i in range(len(PARTS))]
    for name in issue_order(chips // 2):
        index = int(name[-1])
        if name[0] == "W":
            begin, heads = PARTS[index]
            held = (tied(w_out), w_other[0])
            weights[index], before[0] = load("load_weights", 40, held, begin * GROUP * HD, heads * GROUP * HD)
        else:
            next(running[index])
    mine, theirs = sums[0]
    other = cross(theirs)
    return place(order, rows, pad, 1, other, place(order, rows, pad, 0, mine))


def solution(mesh):
    in_specs = (
        P("groups", "gx"),
        P("gx"),
        P("gx", None),
        P(None, "gx"),
        P(("groups", "gx"), None, None),
        P(("groups", "gx"), None, None),
        P(("groups", "gx")),
    )
    out_specs = P("groups", "gx")
    return jax.shard_map(
        functools.partial(per_device, chip_cycle(mesh)), mesh=mesh, in_specs=in_specs, out_specs=out_specs, check_vma=False
    )
```

```python
import functools

import jax
import jax.numpy as jnp
import numpy as np
from jax import lax
from jax.experimental import pallas as pl
from jax.experimental.pallas import tpu as pltpu
from jax.sharding import PartitionSpec as P

D = 8192
HEADS = 64
KVH = 8
HD = 128
GROUP = HEADS // KVH
PARTS = ((0, 4), (4, 4))
LOADS_AHEAD = 6
PIECE_GROUPS = (1, 2, 3, 4)
CUTS = 2
MIB = 1 << 20
BF = jnp.bfloat16
F32 = jnp.float32
TOKEN = jax.ShapeDtypeStruct((8, 128), jnp.float32)


def chip_cycle(mesh):
    devices = np.moveaxis(mesh.devices, mesh.axis_names.index("gx"), -1)
    devices = devices.reshape(-1, devices.shape[-1])[0][::2]
    count = len(devices)
    places = [getattr(d, "coords", None) for d in devices]
    if any(p is None for p in places):
        return list(range(count))

    def linked(a, b):
        return sum(abs(int(u) - int(v)) for u, v in zip(places[a], places[b])) == 1

    def extend(path):
        if len(path) == count:
            return path if linked(path[-1], path[0]) else None
        for nxt in range(count):
            if nxt not in path and linked(path[-1], nxt):
                found = extend(path + [nxt])
                if found:
                    return found
        return None

    return extend([0]) or list(range(count))


def hops(index, chips):
    far = chips // 2
    near = chips - 1 - far
    return (near, far) if index % 2 == 0 else (far, near)


def sent_slots(index, chips):
    up, down = hops(index, chips)
    first = [up, chips - down]
    ks = first + [k for k in range(chips) if k not in first]
    return [(k, 0) for k in ks] + [(k, 1) for k in ks]


def gathered_slots(chips):
    return [(k, w) for w in (0, 1) for k in range(chips)]


def split_rows(rows):
    assert rows % 8 == 6
    return rows // 8


def packed_width(rows, width):
    return split_rows(rows) * width + 3 * width // 4


def pack_rest(a):
    row = lax.broadcasted_iota(jnp.int32, (8, HD), 0)
    b, c, d = pltpu.roll(a[1], 6, 0), pltpu.roll(a[2], 4, 0), pltpu.roll(a[3], 2, 0)
    return a[0] + jnp.where(row >= 6, b, 0.0), jnp.where(row < 4, b, c), jnp.where(row < 2, c, d)


def unpack_rest(tiles, q):
    row = lax.broadcasted_iota(jnp.int32, (8, HD), 0)
    first, second, third = tiles
    if q == 0:
        return jnp.where(row < 6, first, 0.0)
    if q == 1:
        return pltpu.roll(jnp.where(row >= 6, first, jnp.where(row < 4, second, 0.0)), 2, 0)
    if q == 2:
        return pltpu.roll(jnp.where(row >= 4, second, jnp.where(row < 2, third, 0.0)), 4, 0)
    return pltpu.roll(jnp.where(row >= 2, third, 0.0), 6, 0)


def pack_tiles(rows, width, lane, tiles, write):
    full = split_rows(rows)
    for i in range(full):
        for q in range(4):
            write(i * width + lane + q * HD, tiles[q][i * 8 : (i + 1) * 8])
    for i, rest in enumerate(pack_rest([a[full * 8 : full * 8 + 8] for a in tiles])):
        write(full * width + lane * 3 // 4 + i * HD, rest)


def unpack_tile(rows, width, lane, read):
    full = split_rows(rows)
    group, q = lane // (4 * HD) * 4 * HD, lane // HD % 4
    rest = [read(full * width + group * 3 // 4 + i * HD) for i in range(3)]
    return jnp.concatenate([read(i * width + lane) for i in range(full)] + [unpack_rest(rest, q)], axis=0)


def slot_devices(order, slots):
    chips = len(order)
    me = lax.axis_index("gx")
    chip, core = me // 2, me % 2
    place = sum(jnp.where(chip == c, p, 0) for p, c in enumerate(order))

    def chip_at(distance):
        at = (place + distance) % chips
        return sum(jnp.where(at == p, c, 0) for p, c in enumerate(order))

    at = {m: chip_at(m) for m in sorted({m for m, _ in slots})}
    return [at[m] * 2 + jnp.where(core == w, 0, 1) for m, w in slots]


def picker(order, slots, rows, pad, total):
    row = lax.broadcasted_iota(jnp.int32, (pad, total), 0)
    col = lax.broadcasted_iota(jnp.int32, (pad, total), 1)
    picks = [jnp.where((col == row + dev * rows) & (row < rows), 1.0, 0.0) for dev in slot_devices(order, slots)]
    return jnp.concatenate(picks, axis=0).astype(BF)


def qkv_kernel(order, index, rows, pad, x_ref, gain_ref, w_ref, *refs):
    out_refs, (token, xs_ref, x_buf, gain_buf, w_buf, in_sem) = refs[:4], refs[4:]
    token[...] = jnp.zeros_like(token)
    total, depth = x_ref.shape
    begin, heads = PARTS[index]
    piece = heads * HD
    pieces = GROUP + 2
    firsts = [begin * GROUP * HD + j * piece for j in range(GROUP)]
    firsts += [(HEADS + begin) * HD, (HEADS + KVH + begin) * HD]
    slots = sent_slots(index, len(order))
    def load(j):
        lanes = pl.ds(j * piece, piece)
        return pltpu.make_async_copy(w_ref.at[:, pl.ds(firsts[j], piece)], w_buf.at[:, lanes], in_sem.at[j])

    where = [(ref, at) for ref in out_refs for at in range(ref.shape[0])]

    def write(slot, lane, value):
        ref, at = where[slot]
        ref[at, :, lane : lane + HD] = value.astype(BF)

    small = [
        pltpu.make_async_copy(x_ref, x_buf, in_sem.at[pieces]),
        pltpu.make_async_copy(gain_ref, gain_buf, in_sem.at[pieces + 1]),
    ]
    for copy in small:
        copy.start()
    for j in range(LOADS_AHEAD):
        load(j).start()
    pick = picker(order, slots, rows, pad, total)
    for copy in small:
        copy.wait()
    features = jnp.dot(pick, x_buf[...], preferred_element_type=F32)
    xs_ref[...] = (features * gain_buf[...]).astype(BF)
    width = pieces * piece
    packed = packed_width(rows, width)
    extra = (out_refs[0].shape[2] - packed) // 3
    if extra:
        me = lax.axis_index("gx")
        square = jnp.sum(features * features, axis=1, keepdims=True)
        lane = lax.broadcasted_iota(jnp.int32, (len(slots) * pad, extra), 1)
        high = square.astype(BF).astype(F32)
        mid = (square - high).astype(BF).astype(F32)
        low = square - high - mid
        held = jnp.where(lane == 3 * me, high, 0.0) + jnp.where(lane == 3 * me + 1, mid, 0.0) + jnp.where(lane == 3 * me + 2, low, 0.0)
        for slot in range(len(slots)):
            for i in range(3):
                write(slot, packed + i * extra, held[slot * pad + i * 8 : slot * pad + i * 8 + 8])
    done = 0
    for group in PIECE_GROUPS:
        for j in range(done, done + group):
            if j + LOADS_AHEAD < pieces:
                load(j + LOADS_AHEAD).start()
            load(j).wait()
        lanes = slice(done * piece, (done + group) * piece)
        out = jnp.dot(xs_ref[...], w_buf[:, lanes], preferred_element_type=F32)
        for slot in range(len(slots)):
            block = out[slot * pad : (slot + 1) * pad]
            for lane in range(0, group * piece, 4 * HD):
                tiles = [block[:, lane + q * HD : lane + (q + 1) * HD] for q in range(4)]
                pack_tiles(rows, width, done * piece + lane, tiles, functools.partial(write, slot))
        done += group


def project(order, index, rows, pad, x, gain, w):
    piece = PARTS[index][1] * HD
    pieces = GROUP + 2
    depth = x.shape[1]
    chips = len(order)
    extra = -(-6 * chips // 128) * 128 if index == 0 else 0
    width = packed_width(rows, pieces * piece) + 3 * extra
    vmem = pl.BlockSpec(memory_space=pltpu.VMEM)
    return pl.pallas_call(
        functools.partial(qkv_kernel, order, index, rows, pad),
        in_specs=[pl.BlockSpec(memory_space=pltpu.HBM)] * 3,
        out_specs=[vmem] * 5,
        scratch_shapes=[
            pltpu.VMEM((2 * chips * pad, depth), BF),
            pltpu.VMEM(x.shape, BF),
            pltpu.VMEM(gain.shape, F32),
            pltpu.VMEM((depth, pieces * piece), BF),
            pltpu.SemaphoreType.DMA((pieces + 2,)),
        ],
        out_shape=[jax.ShapeDtypeStruct((n, 8, width), BF) for n in (2, chips - 2, 2, chips - 2)] + [TOKEN],
        compiler_params=pltpu.CompilerParams(vmem_limit_bytes=51 * MIB),
        cost_estimate=pl.CostEstimate(flops=1, bytes_accessed=1, transcendentals=0),
        name="qkv_part",
    )(x, gain, w)


def attend_kernel(part, rows, pad, own_ref, left_ref, right_ref, inv_ref, cos_ref, sin_ref, len_ref, k_ref, v_ref, out_ref, s_ref, m_ref, k_buf, v_buf, sems):
    begin, heads = part
    live = rows * GROUP
    full = pad * GROUP
    slots = k_ref.shape[1]
    scale = 1.0 / HD**0.5
    cuts = [rows * i // CUTS for i in range(CUTS + 1)]

    def load(i, which):
        source, target = ((k_ref, k_buf), (v_ref, v_buf))[which]
        seqs = pl.ds(cuts[i], cuts[i + 1] - cuts[i])
        lanes = pl.ds(begin * HD, heads * HD)
        return pltpu.make_async_copy(source.at[seqs, :, lanes], target.at[seqs], sems.at[2 * i + which])

    for which in range(2):
        for i in range(CUTS):
            load(i, which).start()
    inv = inv_ref[...]
    cos = cos_ref[...]
    sin = sin_ref[...]

    def summed(lane):
        lanes = slice(lane, lane + HD)
        got = own_ref[0, :, lanes].astype(F32)
        return got + (left_ref[0, :, lanes].astype(F32) + right_ref[0, :, lanes].astype(F32))

    def tile(t):
        return unpack_tile(rows, (GROUP + 2) * heads * HD, t * HD, summed) * inv

    def turned(t):
        a = tile(t)
        return (a * cos + pltpu.roll(a, HD // 2, 1) * sin).astype(BF)

    r = lax.broadcasted_iota(jnp.int32, (full, full), 0)
    c = lax.broadcasted_iota(jnp.int32, (full, full), 1)
    by_seq = jnp.where(c == (r % GROUP) * pad + r // GROUP, 1.0, 0.0).astype(BF)
    by_head = jnp.where(r == (c % GROUP) * pad + c // GROUP, 1.0, 0.0).astype(BF)
    r2 = lax.broadcasted_iota(jnp.int32, (full, pad), 0)
    c2 = lax.broadcasted_iota(jnp.int32, (full, pad), 1)
    spread = jnp.where(c2 == r2 // GROUP, 1.0, 0.0).astype(BF)
    valid = lax.broadcasted_iota(jnp.int32, (live, slots), 1) < len_ref[...]

    def write(lane, value):
        out_ref[0, :, lane : lane + HD] = value.astype(BF)

    queries, owns, values_new = [], [], []
    for kk in range(heads):
        q = jnp.concatenate([turned(kk * GROUP + g).astype(F32) for g in range(GROUP)], axis=0).astype(BF)
        q = jnp.dot(by_seq, q, preferred_element_type=F32)
        k_new = jnp.dot(spread, turned(heads * GROUP + kk), preferred_element_type=F32)
        values_new.append(jnp.dot(spread, tile(heads * GROUP + heads + kk).astype(BF), preferred_element_type=F32)[:live])
        owns.append((jnp.sum(q * k_new, axis=1, keepdims=True) * scale)[:live])
        queries.append(q)
    for i in range(CUTS):
        load(i, 0).wait()
        for kk in range(heads):
            for s in range(cuts[i], cuts[i + 1]):
                s_ref[kk, s * GROUP : (s + 1) * GROUP] = lax.dot_general(
                    queries[kk][s * GROUP : (s + 1) * GROUP].astype(BF),
                    k_buf[s, :, kk * HD : (kk + 1) * HD],
                    (((1,), (1,)), ((), ())),
                    preferred_element_type=F32,
                )
    own_weights = []
    for kk in range(heads):
        scores = jnp.where(valid, s_ref[kk] * scale, -1e30)
        top = jnp.maximum(jnp.max(scores, axis=1, keepdims=True), owns[kk])
        expo = jnp.where(valid, jnp.exp(scores - top), 0.0)
        own_expo = jnp.exp(owns[kk] - top)
        total = jnp.sum(expo, axis=1, keepdims=True) + own_expo
        s_ref[kk] = expo / total
        own_weights.append((own_expo / total).astype(BF).astype(F32))
    for i in range(CUTS):
        load(i, 1).wait()
        for kk in range(heads):
            for s in range(cuts[i], cuts[i + 1]):
                m_ref[kk, s * GROUP : (s + 1) * GROUP] = jnp.dot(
                    s_ref[kk, s * GROUP : (s + 1) * GROUP].astype(BF),
                    v_buf[s, :, kk * HD : (kk + 1) * HD],
                    preferred_element_type=F32,
                )
    for kk in range(heads):
        mixed = m_ref[kk] + own_weights[kk] * values_new[kk]
        mixed = jnp.concatenate([mixed, jnp.zeros((full - live, HD), F32)], axis=0).astype(BF)
        mixed = jnp.dot(by_head, mixed, preferred_element_type=F32)
        tiles = [mixed[g * pad : (g + 1) * pad] for g in range(GROUP)]
        for g in range(0, GROUP, 4):
            pack_tiles(rows, heads * GROUP * HD, (kk * GROUP + g) * HD, tiles[g : g + 4], write)


def load(name, limit, arrays, begin=0, count=None):
    count = arrays[0].shape[0] if count is None else count

    def kernel(*refs):
        token, sems = refs[-2:]
        copies = [
            pltpu.make_async_copy(refs[i].at[pl.ds(begin, count)], refs[len(arrays) + i], sems.at[i]) for i in range(len(arrays))
        ]
        for copy in copies:
            copy.start()
        for copy in copies:
            copy.wait()
        token[...] = jnp.zeros_like(token)

    *held, token = pl.pallas_call(
        kernel,
        in_specs=[pl.BlockSpec(memory_space=pltpu.HBM)] * len(arrays),
        out_specs=[pl.BlockSpec(memory_space=pltpu.VMEM)] * (len(arrays) + 1),
        out_shape=[jax.ShapeDtypeStruct((count,) + a.shape[1:], BF) for a in arrays] + [TOKEN],
        scratch_shapes=[pltpu.SemaphoreType.DMA((len(arrays),))],
        compiler_params=pltpu.CompilerParams(vmem_limit_bytes=limit * MIB),
        cost_estimate=pl.CostEstimate(flops=1, bytes_accessed=1, transcendentals=0),
        name=name,
    )(*arrays)
    return held, token


def attend(part, rows, pad, own, from_left, from_right, inv, cos, sin, lens, keys, values):
    slots = keys.shape[1]
    heads = part[1]
    vmem = pl.BlockSpec(memory_space=pltpu.VMEM)
    return pl.pallas_call(
        functools.partial(attend_kernel, part, rows, pad),
        in_specs=[vmem] * 7 + [pl.BlockSpec(memory_space=pltpu.HBM)] * 2,
        out_specs=vmem,
        out_shape=jax.ShapeDtypeStruct((1, 8, packed_width(rows, heads * GROUP * HD)), BF),
        scratch_shapes=[
            pltpu.VMEM((heads, rows * GROUP, slots), F32),
            pltpu.VMEM((heads, rows * GROUP, HD), F32),
            pltpu.VMEM((rows, slots, heads * HD), BF),
            pltpu.VMEM((rows, slots, heads * HD), BF),
            pltpu.SemaphoreType.DMA((2 * CUTS,)),
        ],
        compiler_params=pltpu.CompilerParams(vmem_limit_bytes=51 * MIB),
        cost_estimate=pl.CostEstimate(flops=1, bytes_accessed=1, transcendentals=0),
        name="attend_part",
    )(own, from_left, from_right, inv, cos, sin, lens, keys, values)


def features_kernel(order, rows, pad, x_ref, x_other_ref, mine_ref, theirs_ref):
    slots = gathered_slots(len(order))
    pick = picker(order, slots[: len(order)], rows, pad, x_ref.shape[0])
    mine_ref[...] = jnp.dot(pick, x_ref[...], preferred_element_type=F32)
    theirs_ref[...] = jnp.dot(pick, x_other_ref[...], preferred_element_type=F32)


def features_of(order, rows, pad, x, x_other):
    vmem = pl.BlockSpec(memory_space=pltpu.VMEM)
    return pl.pallas_call(
        functools.partial(features_kernel, order, rows, pad),
        in_specs=[vmem] * 2,
        out_specs=[vmem] * 2,
        out_shape=[jax.ShapeDtypeStruct((len(order) * pad, x.shape[1]), F32)] * 2,
        compiler_params=pltpu.CompilerParams(vmem_limit_bytes=8 * MIB),
        cost_estimate=pl.CostEstimate(flops=1, bytes_accessed=1, transcendentals=0),
        name="features",
    )(x, x_other)


def out_kernel(rows, pad, *refs):
    outs, a_ref = refs[-3:-1], refs[-1]
    priors, weights, blocks = refs[-5:-3], refs[-7:-5], refs[:-7]
    width = weights[0].shape[0]
    for b, block in enumerate(blocks):
        for lane in range(0, width, HD):
            tile = unpack_tile(rows, width, lane, lambda at: block[0, :, at : at + HD].astype(F32))
            a_ref[b * pad : (b + 1) * pad, lane : lane + HD] = tile
    left = a_ref[...].astype(BF)
    for w_ref, prior_ref, out_ref in zip(weights, priors, outs):
        out_ref[...] = (prior_ref[...] + jnp.dot(left, w_ref[...], preferred_element_type=F32)).astype(out_ref.dtype)


def project_out(rows, pad, blocks, weights, prior, dtype):
    count = len(blocks)
    depth, cols = weights[0].shape
    vmem = pl.BlockSpec(memory_space=pltpu.VMEM)
    args = [*blocks, *weights, *prior]
    return pl.pallas_call(
        functools.partial(out_kernel, rows, pad),
        in_specs=[vmem] * len(args),
        out_specs=[vmem] * 2,
        scratch_shapes=[pltpu.VMEM((count * pad, depth), F32)],
        out_shape=[jax.ShapeDtypeStruct((count * pad, cols), dtype)] * 2,
        compiler_params=pltpu.CompilerParams(vmem_limit_bytes=12 * MIB),
        cost_estimate=pl.CostEstimate(flops=1, bytes_accessed=1, transcendentals=0),
        name="out_part",
    )(*args)


def place_kernel(order, rows, pad, which, rows_ref, *refs):
    out_ref = refs[-1]
    chips = len(order)
    pick = picker(order, gathered_slots(chips)[which * chips : (which + 1) * chips], rows, pad, out_ref.shape[0])
    placed = lax.dot_general(pick, rows_ref[...], (((0,), (0,)), ((), ())), preferred_element_type=F32)
    if len(refs) > 1:
        placed = placed + refs[0][...].astype(F32)
    out_ref[...] = placed.astype(BF)


def place(order, rows, pad, which, result, *other):
    vmem = pl.BlockSpec(memory_space=pltpu.VMEM)
    return pl.pallas_call(
        functools.partial(place_kernel, order, rows, pad, which),
        in_specs=[vmem] * (1 + len(other)),
        out_specs=vmem,
        out_shape=jax.ShapeDtypeStruct((2 * len(order) * rows, result.shape[1]), BF),
        compiler_params=pltpu.CompilerParams(vmem_limit_bytes=8 * MIB),
        cost_estimate=pl.CostEstimate(flops=1, bytes_accessed=1, transcendentals=0),
        name="place",
    )(result, *other)


def wide(a):
    return a.astype(F32)


def issue_order(steps):
    names = ["P0", "R0", "P1", "R0", "R1"] + ["R0", "R1"] * (steps - 2) + ["R1"]
    return names + ["T0", "G0", "T1", "G1", "G0", "W0", "G1", "G0", "W1", "G1"] + ["G0", "G1"] * (steps - 3) + ["O0", "O1"]


def per_device(order, hidden_in, norm_gain, w_qkv, w_out, cache_keys, cache_values, lengths):
    rows = cache_keys.shape[0]
    pad = -(-rows // 8) * 8
    chips = len(order)
    up_pairs = [(order[p] * 2 + c, order[(p + 1) % chips] * 2 + c) for p in range(chips) for c in range(2)]
    down_pairs = [(b, a) for a, b in up_pairs]
    sibling = [(i, i ^ 1) for i in range(2 * chips)]
    before = [None]

    def after(a, *others):
        return lax.optimization_barrier((a,) + others)[0]

    def ring(sent):
        before[0] = tuple(sent.values())
        return {way: lax.ppermute(a, "gx", up_pairs if way == "up" else down_pairs) for way, a in sent.items()}

    def tied(a):
        return after(a, before[0])

    def cross(a):
        return lax.ppermute(a, "gx", sibling)

    def positions(lengths):
        angles = HD // 2
        inverse = 500000.0 ** (-(jnp.arange(angles, dtype=F32) * 2.0 / HD))
        angle = jnp.pad(lengths, (0, pad - rows)).astype(F32)[:, None] * inverse[None, :]
        cos = jnp.cos(angle)
        sin = jnp.sin(angle)
        return jnp.concatenate([cos, cos], axis=1), jnp.concatenate([-sin, sin], axis=1), jnp.repeat(lengths, GROUP)[:, None]

    gain = norm_gain[None, :]
    inv, w_other, x_other, places, sums, weights = [None], [None], [None], [None], [None], {}

    def part_steps(index):
        part = PARTS[index]
        ways = dict(zip(("up", "down"), hops(index, chips)))
        steps = max(ways.values())
        sign = {"up": 1, "down": -1}
        ks = [k for k, w in sent_slots(index, chips) if w == 0]
        x = hidden_in if index == 0 else tied(hidden_in)
        keep_first, keep_rest, first, rest, before[0] = project(order, index, rows, pad, x, gain, w_qkv)
        got_first = cross(first)
        got_rest = cross(rest)
        yield

        front = (wide(tied(keep_first)) + wide(got_first)).astype(BF)
        back = []

        def piece(k):
            at = ks.index(k % chips)
            if at < 2:
                return front[at : at + 1]
            if not back:
                back.append((wide(keep_rest) + wide(got_rest)).astype(BF))
            return back[0][at - 2 : at - 1]

        moved = {}
        for step in range(steps):
            sent = {}
            for way, far in ways.items():
                if step < far:
                    sent[way] = piece(sign[way] * (far - step))
                    if step:
                        sent[way] = (wide(sent[way]) + wide(tied(moved[way]))).astype(BF)
            moved = {**moved, **ring(sent)}
            if index == 1 and step == 1:
                w_other[0] = cross(tied(w_out))
                x_other[0] = cross(tied(hidden_in))
            if index == 1 and step == 2:
                places[0] = positions(tied(lengths))
                sums[0] = features_of(order, rows, pad, hidden_in, x_other[0])
            yield
        own = piece(0)
        if index == 0:
            first = packed_width(rows, (GROUP + 2) * part[1] * HD)
            terms = sum(wide(a[0, :, first:]) for a in (own, moved["up"], moved["down"]))
            square = jnp.sum(terms.reshape(8, 3, -1), axis=2).T.reshape(pad)
            inv[0] = jnp.broadcast_to(lax.rsqrt(square / D + 1e-05)[:, None], (pad, HD))
        own = tied(own)
        if index == 0:
            own = after(own, x_other[0])
        if index == 1 and 1 not in weights:
            own = after(own, w_other[0])
        attended = attend(part, rows, pad, own, moved["up"], moved["down"], inv[0], *places[0], cache_keys, cache_values)
        before[0] = attended
        yield
        blocks = {0: attended}
        for step in range(steps):
            sent = {way: tied(blocks[-sign[way] * step % chips]) for way, far in ways.items() if step < far}
            for way, a in ring(sent).items():
                blocks[-sign[way] * (step + 1) % chips] = a
            yield
        last = index == len(PARTS) - 1
        sums[0] = project_out(rows, pad, [blocks[k] for k in range(chips)], weights[index], sums[0], BF if last else F32)
        yield

    running = [part_steps(i) for i in range(len(PARTS))]
    for name in issue_order(chips // 2):
        index = int(name[-1])
        if name[0] == "W":
            begin, heads = PARTS[index]
            held = (tied(w_out), w_other[0])
            weights[index], before[0] = load("load_weights", 40, held, begin * GROUP * HD, heads * GROUP * HD)
        else:
            next(running[index])
    mine, theirs = sums[0]
    other = cross(theirs)
    return place(order, rows, pad, 1, other, place(order, rows, pad, 0, mine))


def solution(mesh):
    in_specs = (
        P("groups", "gx"),
        P("gx"),
        P("gx", None),
        P(None, "gx"),
        P(("groups", "gx"), None, None),
        P(("groups", "gx"), None, None),
        P(("groups", "gx")),
    )
    out_specs = P("groups", "gx")
    return jax.shard_map(
        functools.partial(per_device, chip_cycle(mesh)), mesh=mesh, in_specs=in_specs, out_specs=out_specs, check_vma=False
    )
```

```python
import functools

import jax
import jax.numpy as jnp
import numpy as np
from jax import lax
from jax.experimental import pallas as pl
from jax.experimental.pallas import tpu as pltpu
from jax.sharding import PartitionSpec as P

D = 8192
HEADS = 64
KVH = 8
HD = 128
GROUP = HEADS // KVH
PARTS = ((0, 4), (4, 4))
LOADS_AHEAD = 6
PIECE_GROUPS = (2, 3, 3, 2)
CUTS = 2
MIB = 1 << 20
BF = jnp.bfloat16
F32 = jnp.float32
TOKEN = jax.ShapeDtypeStruct((8, 128), jnp.float32)


def chip_cycle(mesh):
    devices = np.moveaxis(mesh.devices, mesh.axis_names.index("gx"), -1)
    devices = devices.reshape(-1, devices.shape[-1])[0][::2]
    count = len(devices)
    places = [getattr(d, "coords", None) for d in devices]
    if any(p is None for p in places):
        return list(range(count))

    def linked(a, b):
        return sum(abs(int(u) - int(v)) for u, v in zip(places[a], places[b])) == 1

    def extend(path):
        if len(path) == count:
            return path if linked(path[-1], path[0]) else None
        for nxt in range(count):
            if nxt not in path and linked(path[-1], nxt):
                found = extend(path + [nxt])
                if found:
                    return found
        return None

    return extend([0]) or list(range(count))


def hops(index, chips):
    far = chips // 2
    near = chips - 1 - far
    return (near, far) if index % 2 == 0 else (far, near)


def sent_slots(index, chips):
    up, down = hops(index, chips)
    first = [up, chips - down]
    ks = first + [k for k in range(chips) if k not in first]
    return [(k, 0) for k in ks] + [(k, 1) for k in ks]


def gathered_slots(chips):
    return [(k, w) for w in (0, 1) for k in range(chips)]


def split_rows(rows):
    assert rows % 8 == 6
    return rows // 8


def packed_width(rows, width):
    return split_rows(rows) * width + 3 * width // 4


def pack_rest(a):
    row = lax.broadcasted_iota(jnp.int32, (8, HD), 0)
    b, c, d = pltpu.roll(a[1], 6, 0), pltpu.roll(a[2], 4, 0), pltpu.roll(a[3], 2, 0)
    return a[0] + jnp.where(row >= 6, b, 0.0), jnp.where(row < 4, b, c), jnp.where(row < 2, c, d)


def unpack_rest(tiles, q):
    row = lax.broadcasted_iota(jnp.int32, (8, HD), 0)
    first, second, third = tiles
    if q == 0:
        return jnp.where(row < 6, first, 0.0)
    if q == 1:
        return pltpu.roll(jnp.where(row >= 6, first, jnp.where(row < 4, second, 0.0)), 2, 0)
    if q == 2:
        return pltpu.roll(jnp.where(row >= 4, second, jnp.where(row < 2, third, 0.0)), 4, 0)
    return pltpu.roll(jnp.where(row >= 2, third, 0.0), 6, 0)


def pack_tiles(rows, width, lane, tiles, write):
    full = split_rows(rows)
    for i in range(full):
        for q in range(4):
            write(i * width + lane + q * HD, tiles[q][i * 8 : (i + 1) * 8])
    for i, rest in enumerate(pack_rest([a[full * 8 : full * 8 + 8] for a in tiles])):
        write(full * width + lane * 3 // 4 + i * HD, rest)


def unpack_tile(rows, width, lane, read):
    full = split_rows(rows)
    group, q = lane // (4 * HD) * 4 * HD, lane // HD % 4
    rest = [read(full * width + group * 3 // 4 + i * HD) for i in range(3)]
    return jnp.concatenate([read(i * width + lane) for i in range(full)] + [unpack_rest(rest, q)], axis=0)


def slot_devices(order, slots):
    chips = len(order)
    me = lax.axis_index("gx")
    chip, core = me // 2, me % 2
    place = sum(jnp.where(chip == c, p, 0) for p, c in enumerate(order))

    def chip_at(distance):
        at = (place + distance) % chips
        return sum(jnp.where(at == p, c, 0) for p, c in enumerate(order))

    at = {m: chip_at(m) for m in sorted({m for m, _ in slots})}
    return [at[m] * 2 + jnp.where(core == w, 0, 1) for m, w in slots]


def picker(order, slots, rows, pad, total):
    row = lax.broadcasted_iota(jnp.int32, (pad, total), 0)
    col = lax.broadcasted_iota(jnp.int32, (pad, total), 1)
    picks = [jnp.where((col == row + dev * rows) & (row < rows), 1.0, 0.0) for dev in slot_devices(order, slots)]
    return jnp.concatenate(picks, axis=0).astype(BF)


def qkv_kernel(order, index, rows, pad, x_ref, gain_ref, w_ref, *refs):
    out_refs, (token, xs_ref, x_buf, gain_buf, w_buf, in_sem) = refs[:4], refs[4:]
    token[...] = jnp.zeros_like(token)
    total, depth = x_ref.shape
    begin, heads = PARTS[index]
    piece = heads * HD
    pieces = GROUP + 2
    firsts = [begin * GROUP * HD + j * piece for j in range(GROUP)]
    firsts += [(HEADS + begin) * HD, (HEADS + KVH + begin) * HD]
    slots = sent_slots(index, len(order))
    def load(j):
        lanes = pl.ds(j * piece, piece)
        return pltpu.make_async_copy(w_ref.at[:, pl.ds(firsts[j], piece)], w_buf.at[:, lanes], in_sem.at[j])

    where = [(ref, at) for ref in out_refs for at in range(ref.shape[0])]

    def write(slot, lane, value):
        ref, at = where[slot]
        ref[at, :, lane : lane + HD] = value.astype(BF)

    small = [
        pltpu.make_async_copy(x_ref, x_buf, in_sem.at[pieces]),
        pltpu.make_async_copy(gain_ref, gain_buf, in_sem.at[pieces + 1]),
    ]
    for copy in small:
        copy.start()
    for j in range(LOADS_AHEAD):
        load(j).start()
    pick = picker(order, slots, rows, pad, total)
    for copy in small:
        copy.wait()
    features = jnp.dot(pick, x_buf[...], preferred_element_type=F32)
    xs_ref[...] = (features * gain_buf[...]).astype(BF)
    width = pieces * piece
    packed = packed_width(rows, width)
    extra = (out_refs[0].shape[2] - packed) // 3
    if extra:
        me = lax.axis_index("gx")
        square = jnp.sum(features * features, axis=1, keepdims=True)
        lane = lax.broadcasted_iota(jnp.int32, (len(slots) * pad, extra), 1)
        high = square.astype(BF).astype(F32)
        mid = (square - high).astype(BF).astype(F32)
        low = square - high - mid
        held = jnp.where(lane == 3 * me, high, 0.0) + jnp.where(lane == 3 * me + 1, mid, 0.0) + jnp.where(lane == 3 * me + 2, low, 0.0)
        for slot in range(len(slots)):
            for i in range(3):
                write(slot, packed + i * extra, held[slot * pad + i * 8 : slot * pad + i * 8 + 8])
    done = 0
    for group in PIECE_GROUPS:
        for j in range(done, done + group):
            if j + LOADS_AHEAD < pieces:
                load(j + LOADS_AHEAD).start()
            load(j).wait()
        lanes = slice(done * piece, (done + group) * piece)
        out = jnp.dot(xs_ref[...], w_buf[:, lanes], preferred_element_type=F32)
        for slot in range(len(slots)):
            block = out[slot * pad : (slot + 1) * pad]
            for lane in range(0, group * piece, 4 * HD):
                tiles = [block[:, lane + q * HD : lane + (q + 1) * HD] for q in range(4)]
                pack_tiles(rows, width, done * piece + lane, tiles, functools.partial(write, slot))
        done += group


def project(order, index, rows, pad, x, gain, w):
    piece = PARTS[index][1] * HD
    pieces = GROUP + 2
    depth = x.shape[1]
    chips = len(order)
    extra = -(-6 * chips // 128) * 128 if index == 0 else 0
    width = packed_width(rows, pieces * piece) + 3 * extra
    vmem = pl.BlockSpec(memory_space=pltpu.VMEM)
    return pl.pallas_call(
        functools.partial(qkv_kernel, order, index, rows, pad),
        in_specs=[pl.BlockSpec(memory_space=pltpu.HBM)] * 3,
        out_specs=[vmem] * 5,
        scratch_shapes=[
            pltpu.VMEM((2 * chips * pad, depth), BF),
            pltpu.VMEM(x.shape, BF),
            pltpu.VMEM(gain.shape, F32),
            pltpu.VMEM((depth, pieces * piece), BF),
            pltpu.SemaphoreType.DMA((pieces + 2,)),
        ],
        out_shape=[jax.ShapeDtypeStruct((n, 8, width), BF) for n in (2, chips - 2, 2, chips - 2)] + [TOKEN],
        compiler_params=pltpu.CompilerParams(vmem_limit_bytes=51 * MIB),
        cost_estimate=pl.CostEstimate(flops=1, bytes_accessed=1, transcendentals=0),
        name="qkv_part",
    )(x, gain, w)


def attend_kernel(part, rows, pad, own_ref, left_ref, right_ref, inv_ref, cos_ref, sin_ref, len_ref, k_ref, v_ref, out_ref, s_ref, m_ref, k_buf, v_buf, sems):
    begin, heads = part
    live = rows * GROUP
    full = pad * GROUP
    slots = k_ref.shape[1]
    scale = 1.0 / HD**0.5
    cuts = [rows * i // CUTS for i in range(CUTS + 1)]

    def load(i, which):
        source, target = ((k_ref, k_buf), (v_ref, v_buf))[which]
        seqs = pl.ds(cuts[i], cuts[i + 1] - cuts[i])
        lanes = pl.ds(begin * HD, heads * HD)
        return pltpu.make_async_copy(source.at[seqs, :, lanes], target.at[seqs], sems.at[2 * i + which])

    for which in range(2):
        for i in range(CUTS):
            load(i, which).start()
    inv = inv_ref[...]
    cos = cos_ref[...]
    sin = sin_ref[...]

    def summed(lane):
        lanes = slice(lane, lane + HD)
        got = own_ref[0, :, lanes].astype(F32)
        return got + (left_ref[0, :, lanes].astype(F32) + right_ref[0, :, lanes].astype(F32))

    def tile(t):
        return unpack_tile(rows, (GROUP + 2) * heads * HD, t * HD, summed) * inv

    def turned(t):
        a = tile(t)
        return (a * cos + pltpu.roll(a, HD // 2, 1) * sin).astype(BF)

    r = lax.broadcasted_iota(jnp.int32, (full, full), 0)
    c = lax.broadcasted_iota(jnp.int32, (full, full), 1)
    by_seq = jnp.where(c == (r % GROUP) * pad + r // GROUP, 1.0, 0.0).astype(BF)
    by_head = jnp.where(r == (c % GROUP) * pad + c // GROUP, 1.0, 0.0).astype(BF)
    r2 = lax.broadcasted_iota(jnp.int32, (full, pad), 0)
    c2 = lax.broadcasted_iota(jnp.int32, (full, pad), 1)
    spread = jnp.where(c2 == r2 // GROUP, 1.0, 0.0).astype(BF)
    valid = lax.broadcasted_iota(jnp.int32, (live, slots), 1) < len_ref[...]

    def write(lane, value):
        out_ref[0, :, lane : lane + HD] = value.astype(BF)

    queries, owns, values_new = [], [], []
    for kk in range(heads):
        q = jnp.concatenate([turned(kk * GROUP + g).astype(F32) for g in range(GROUP)], axis=0).astype(BF)
        q = jnp.dot(by_seq, q, preferred_element_type=F32)
        k_new = jnp.dot(spread, turned(heads * GROUP + kk), preferred_element_type=F32)
        values_new.append(jnp.dot(spread, tile(heads * GROUP + heads + kk).astype(BF), preferred_element_type=F32)[:live])
        owns.append((jnp.sum(q * k_new, axis=1, keepdims=True) * scale)[:live])
        queries.append(q)
    for i in range(CUTS):
        load(i, 0).wait()
        for kk in range(heads):
            for s in range(cuts[i], cuts[i + 1]):
                s_ref[kk, s * GROUP : (s + 1) * GROUP] = lax.dot_general(
                    queries[kk][s * GROUP : (s + 1) * GROUP].astype(BF),
                    k_buf[s, :, kk * HD : (kk + 1) * HD],
                    (((1,), (1,)), ((), ())),
                    preferred_element_type=F32,
                )
    own_weights = []
    for kk in range(heads):
        scores = jnp.where(valid, s_ref[kk] * scale, -1e30)
        top = jnp.maximum(jnp.max(scores, axis=1, keepdims=True), owns[kk])
        expo = jnp.where(valid, jnp.exp(scores - top), 0.0)
        own_expo = jnp.exp(owns[kk] - top)
        total = jnp.sum(expo, axis=1, keepdims=True) + own_expo
        s_ref[kk] = expo / total
        own_weights.append((own_expo / total).astype(BF).astype(F32))
    for i in range(CUTS):
        load(i, 1).wait()
        for kk in range(heads):
            for s in range(cuts[i], cuts[i + 1]):
                m_ref[kk, s * GROUP : (s + 1) * GROUP] = jnp.dot(
                    s_ref[kk, s * GROUP : (s + 1) * GROUP].astype(BF),
                    v_buf[s, :, kk * HD : (kk + 1) * HD],
                    preferred_element_type=F32,
                )
    for kk in range(heads):
        mixed = m_ref[kk] + own_weights[kk] * values_new[kk]
        mixed = jnp.concatenate([mixed, jnp.zeros((full - live, HD), F32)], axis=0).astype(BF)
        mixed = jnp.dot(by_head, mixed, preferred_element_type=F32)
        tiles = [mixed[g * pad : (g + 1) * pad] for g in range(GROUP)]
        for g in range(0, GROUP, 4):
            pack_tiles(rows, heads * GROUP * HD, (kk * GROUP + g) * HD, tiles[g : g + 4], write)


def load(name, limit, arrays, begin=0, count=None):
    count = arrays[0].shape[0] if count is None else count

    def kernel(*refs):
        token, sems = refs[-2:]
        copies = [
            pltpu.make_async_copy(refs[i].at[pl.ds(begin, count)], refs[len(arrays) + i], sems.at[i]) for i in range(len(arrays))
        ]
        for copy in copies:
            copy.start()
        for copy in copies:
            copy.wait()
        token[...] = jnp.zeros_like(token)

    *held, token = pl.pallas_call(
        kernel,
        in_specs=[pl.BlockSpec(memory_space=pltpu.HBM)] * len(arrays),
        out_specs=[pl.BlockSpec(memory_space=pltpu.VMEM)] * (len(arrays) + 1),
        out_shape=[jax.ShapeDtypeStruct((count,) + a.shape[1:], BF) for a in arrays] + [TOKEN],
        scratch_shapes=[pltpu.SemaphoreType.DMA((len(arrays),))],
        compiler_params=pltpu.CompilerParams(vmem_limit_bytes=limit * MIB),
        cost_estimate=pl.CostEstimate(flops=1, bytes_accessed=1, transcendentals=0),
        name=name,
    )(*arrays)
    return held, token


def attend(part, rows, pad, own, from_left, from_right, inv, cos, sin, lens, keys, values):
    slots = keys.shape[1]
    heads = part[1]
    vmem = pl.BlockSpec(memory_space=pltpu.VMEM)
    return pl.pallas_call(
        functools.partial(attend_kernel, part, rows, pad),
        in_specs=[vmem] * 7 + [pl.BlockSpec(memory_space=pltpu.HBM)] * 2,
        out_specs=vmem,
        out_shape=jax.ShapeDtypeStruct((1, 8, packed_width(rows, heads * GROUP * HD)), BF),
        scratch_shapes=[
            pltpu.VMEM((heads, rows * GROUP, slots), F32),
            pltpu.VMEM((heads, rows * GROUP, HD), F32),
            pltpu.VMEM((rows, slots, heads * HD), BF),
            pltpu.VMEM((rows, slots, heads * HD), BF),
            pltpu.SemaphoreType.DMA((2 * CUTS,)),
        ],
        compiler_params=pltpu.CompilerParams(vmem_limit_bytes=51 * MIB),
        cost_estimate=pl.CostEstimate(flops=1, bytes_accessed=1, transcendentals=0),
        name="attend_part",
    )(own, from_left, from_right, inv, cos, sin, lens, keys, values)


def features_kernel(order, rows, pad, x_ref, x_other_ref, mine_ref, theirs_ref):
    slots = gathered_slots(len(order))
    pick = picker(order, slots[: len(order)], rows, pad, x_ref.shape[0])
    mine_ref[...] = jnp.dot(pick, x_ref[...], preferred_element_type=F32)
    theirs_ref[...] = jnp.dot(pick, x_other_ref[...], preferred_element_type=F32)


def features_of(order, rows, pad, x, x_other):
    vmem = pl.BlockSpec(memory_space=pltpu.VMEM)
    return pl.pallas_call(
        functools.partial(features_kernel, order, rows, pad),
        in_specs=[vmem] * 2,
        out_specs=[vmem] * 2,
        out_shape=[jax.ShapeDtypeStruct((len(order) * pad, x.shape[1]), F32)] * 2,
        compiler_params=pltpu.CompilerParams(vmem_limit_bytes=8 * MIB),
        cost_estimate=pl.CostEstimate(flops=1, bytes_accessed=1, transcendentals=0),
        name="features",
    )(x, x_other)


def out_kernel(rows, pad, *refs):
    outs, a_ref = refs[-3:-1], refs[-1]
    priors, weights, blocks = refs[-5:-3], refs[-7:-5], refs[:-7]
    width = weights[0].shape[0]
    for b, block in enumerate(blocks):
        for lane in range(0, width, HD):
            tile = unpack_tile(rows, width, lane, lambda at: block[0, :, at : at + HD].astype(F32))
            a_ref[b * pad : (b + 1) * pad, lane : lane + HD] = tile
    left = a_ref[...].astype(BF)
    for w_ref, prior_ref, out_ref in zip(weights, priors, outs):
        out_ref[...] = (prior_ref[...] + jnp.dot(left, w_ref[...], preferred_element_type=F32)).astype(out_ref.dtype)


def project_out(rows, pad, blocks, weights, prior, dtype):
    count = len(blocks)
    depth, cols = weights[0].shape
    vmem = pl.BlockSpec(memory_space=pltpu.VMEM)
    args = [*blocks, *weights, *prior]
    return pl.pallas_call(
        functools.partial(out_kernel, rows, pad),
        in_specs=[vmem] * len(args),
        out_specs=[vmem] * 2,
        scratch_shapes=[pltpu.VMEM((count * pad, depth), F32)],
        out_shape=[jax.ShapeDtypeStruct((count * pad, cols), dtype)] * 2,
        compiler_params=pltpu.CompilerParams(vmem_limit_bytes=12 * MIB),
        cost_estimate=pl.CostEstimate(flops=1, bytes_accessed=1, transcendentals=0),
        name="out_part",
    )(*args)


def place_kernel(order, rows, pad, which, rows_ref, *refs):
    out_ref = refs[-1]
    chips = len(order)
    pick = picker(order, gathered_slots(chips)[which * chips : (which + 1) * chips], rows, pad, out_ref.shape[0])
    placed = lax.dot_general(pick, rows_ref[...], (((0,), (0,)), ((), ())), preferred_element_type=F32)
    if len(refs) > 1:
        placed = placed + refs[0][...].astype(F32)
    out_ref[...] = placed.astype(BF)


def place(order, rows, pad, which, result, *other):
    vmem = pl.BlockSpec(memory_space=pltpu.VMEM)
    return pl.pallas_call(
        functools.partial(place_kernel, order, rows, pad, which),
        in_specs=[vmem] * (1 + len(other)),
        out_specs=vmem,
        out_shape=jax.ShapeDtypeStruct((2 * len(order) * rows, result.shape[1]), BF),
        compiler_params=pltpu.CompilerParams(vmem_limit_bytes=8 * MIB),
        cost_estimate=pl.CostEstimate(flops=1, bytes_accessed=1, transcendentals=0),
        name="place",
    )(result, *other)


def wide(a):
    return a.astype(F32)


def issue_order(steps):
    names = ["P0", "R0", "P1", "R0", "R1"] + ["R0", "R1"] * (steps - 2) + ["R1"]
    return names + ["T0", "G0", "T1", "G1", "G0", "W0", "G1", "G0", "W1", "G1"] + ["G0", "G1"] * (steps - 3) + ["O0", "O1"]


def per_device(order, hidden_in, norm_gain, w_qkv, w_out, cache_keys, cache_values, lengths):
    rows = cache_keys.shape[0]
    pad = -(-rows // 8) * 8
    chips = len(order)
    up_pairs = [(order[p] * 2 + c, order[(p + 1) % chips] * 2 + c) for p in range(chips) for c in range(2)]
    down_pairs = [(b, a) for a, b in up_pairs]
    sibling = [(i, i ^ 1) for i in range(2 * chips)]
    before = [None]

    def after(a, *others):
        return lax.optimization_barrier((a,) + others)[0]

    def ring(sent):
        before[0] = tuple(sent.values())
        return {way: lax.ppermute(a, "gx", up_pairs if way == "up" else down_pairs) for way, a in sent.items()}

    def tied(a):
        return after(a, before[0])

    def cross(a):
        return lax.ppermute(a, "gx", sibling)

    def positions(lengths):
        angles = HD // 2
        inverse = 500000.0 ** (-(jnp.arange(angles, dtype=F32) * 2.0 / HD))
        angle = jnp.pad(lengths, (0, pad - rows)).astype(F32)[:, None] * inverse[None, :]
        cos = jnp.cos(angle)
        sin = jnp.sin(angle)
        return jnp.concatenate([cos, cos], axis=1), jnp.concatenate([-sin, sin], axis=1), jnp.repeat(lengths, GROUP)[:, None]

    gain = norm_gain[None, :]
    inv, w_other, x_other, places, sums, weights = [None], [None], [None], [None], [None], {}

    def part_steps(index):
        part = PARTS[index]
        ways = dict(zip(("up", "down"), hops(index, chips)))
        steps = max(ways.values())
        sign = {"up": 1, "down": -1}
        ks = [k for k, w in sent_slots(index, chips) if w == 0]
        x = hidden_in if index == 0 else tied(hidden_in)
        keep_first, keep_rest, first, rest, before[0] = project(order, index, rows, pad, x, gain, w_qkv)
        got_first = cross(first)
        got_rest = cross(rest)
        yield

        front = (wide(tied(keep_first)) + wide(got_first)).astype(BF)
        back = []

        def piece(k):
            at = ks.index(k % chips)
            if at < 2:
                return front[at : at + 1]
            if not back:
                back.append((wide(keep_rest) + wide(got_rest)).astype(BF))
            return back[0][at - 2 : at - 1]

        moved = {}
        for step in range(steps):
            sent = {}
            for way, far in ways.items():
                if step < far:
                    sent[way] = piece(sign[way] * (far - step))
                    if step:
                        sent[way] = (wide(sent[way]) + wide(tied(moved[way]))).astype(BF)
            moved = {**moved, **ring(sent)}
            if index == 1 and step == 1:
                w_other[0] = cross(tied(w_out))
                x_other[0] = cross(tied(hidden_in))
            if index == 1 and step == 2:
                places[0] = positions(tied(lengths))
                sums[0] = features_of(order, rows, pad, hidden_in, x_other[0])
            yield
        own = piece(0)
        if index == 0:
            first = packed_width(rows, (GROUP + 2) * part[1] * HD)
            terms = sum(wide(a[0, :, first:]) for a in (own, moved["up"], moved["down"]))
            square = jnp.sum(terms.reshape(8, 3, -1), axis=2).T.reshape(pad)
            inv[0] = jnp.broadcast_to(lax.rsqrt(square / D + 1e-05)[:, None], (pad, HD))
        own = tied(own)
        if index == 0:
            own = after(own, x_other[0])
        if index == 1 and 1 not in weights:
            own = after(own, w_other[0])
        attended = attend(part, rows, pad, own, moved["up"], moved["down"], inv[0], *places[0], cache_keys, cache_values)
        before[0] = attended
        yield
        blocks = {0: attended}
        for step in range(steps):
            sent = {way: tied(blocks[-sign[way] * step % chips]) for way, far in ways.items() if step < far}
            for way, a in ring(sent).items():
                blocks[-sign[way] * (step + 1) % chips] = a
            yield
        last = index == len(PARTS) - 1
        sums[0] = project_out(rows, pad, [blocks[k] for k in range(chips)], weights[index], sums[0], BF if last else F32)
        yield

    running = [part_steps(i) for i in range(len(PARTS))]
    for name in issue_order(chips // 2):
        index = int(name[-1])
        if name[0] == "W":
            begin, heads = PARTS[index]
            held = (tied(w_out), w_other[0])
            weights[index], before[0] = load("load_weights", 40, held, begin * GROUP * HD, heads * GROUP * HD)
        else:
            next(running[index])
    mine, theirs = sums[0]
    other = cross(theirs)
    return place(order, rows, pad, 1, other, place(order, rows, pad, 0, mine))


def solution(mesh):
    in_specs = (
        P("groups", "gx"),
        P("gx"),
        P("gx", None),
        P(None, "gx"),
        P(("groups", "gx"), None, None),
        P(("groups", "gx"), None, None),
        P(("groups", "gx")),
    )
    out_specs = P("groups", "gx")
    return jax.shard_map(
        functools.partial(per_device, chip_cycle(mesh)), mesh=mesh, in_specs=in_specs, out_specs=out_specs, check_vma=False
    )
```
